512 devices in a mesh: row: 32 (over x, y), col: 16 (over z, core).
Axes of the slice: x: 4, y: 8, z: 8, core: 2. Of those that a mesh axis runs over, the one named last changes fastest.
Arguments:
- cov: float32 [2, 8192, 4, 4096], P(None, 'row', None, 'col'), may hold values from 0 to 6, as said below
Outputs:
- factored: float32 [2, 8192, 4, 4096], P(None, 'row', None, 'col')
The draws below stay inside these ranges and needn't reach their ends.
Inputs may be any that keep to these rules, and one draw needn't show every extreme that they name: cov is symmetric positive definite: s_i s_j exp(-|x_i - x_j| / ell) over site positions x in the unit square and positive site scales s, plus a nugget between 0.5 and 1.5 on the diagonal.
All inputs are finite; a program needn't handle non-finite values.
Results may differ from the reference program's by a relative error of at most 0.0003.
Values sent between devices are 32-bit elements; how exact they have to be, the bound alone decides.
No kernel may reach another device: no remote copies, remote signals or barrier semaphores. Data moves between devices by JAX's collectives and lax.ppermute only.
A program may use at most 64 MiB of HBM per device.

```python
import jax
import jax.numpy as jnp
from jax import lax

NB = 256
TRD = 2
TCD = 4
ORDER = 16384
N_ROW = 32
N_COL = 16


def draw_cov(key, part):
    key = jax.random.fold_in(key, 7)
    key_pos, key_scale, key_nugget = jax.random.split(key, 3)
    length = 0.6
    scale_lo = 0.7
    scale_hi = 1.4
    places = jax.random.uniform(key_pos, (ORDER, 2), jnp.float32)
    scales = jnp.exp(jax.random.uniform(key_scale, (ORDER,), jnp.float32, jnp.log(scale_lo), jnp.log(scale_hi)))
    nugget = jax.random.uniform(key_nugget, (ORDER,), jnp.float32, 0.5, 1.5)
    delta_x = places[:, 0][:, None] - places[:, 0][None, :]
    delta_y = places[:, 1][:, None] - places[:, 1][None, :]
    distance = jnp.sqrt(delta_x * delta_x + delta_y * delta_y)
    kernel = scales[:, None] * scales[None, :] * jnp.exp(-distance / length)
    same_site = jnp.arange(ORDER)[:, None] == jnp.arange(ORDER)[None, :]
    matrix = kernel + jnp.where(same_site, nugget[:, None], 0.0)
    return matrix.astype(jnp.float32).reshape(TRD, N_ROW * NB, TCD, N_COL * NB)


def setup_inputs(seed: int = 0) -> dict:
    seeds = jax.random.split(jax.random.key(seed), 2)
    return {
        "cov": draw_cov(jax.random.fold_in(seeds[1], 71), 0),
    }


def reference(cov):
    matrix = cov.reshape(ORDER, ORDER)
    identity = jnp.eye(NB, dtype=jnp.float32)
    for panel_step in range(2):
        first_row = panel_step * NB
        after_row = first_row + NB
        factor_tile = jnp.linalg.cholesky(matrix[first_row:after_row, first_row:after_row])
        inverse = lax.linalg.triangular_solve(factor_tile, identity, left_side=True, lower=True)
        solved = jnp.dot(matrix[after_row:, first_row:after_row], inverse.T, precision=lax.Precision.HIGHEST)
        matrix = matrix.at[after_row:, after_row:].add(-jnp.dot(solved, solved.T, precision=lax.Precision.HIGHEST))
        matrix = matrix.at[first_row:after_row, first_row:after_row].set(factor_tile)
        matrix = matrix.at[after_row:, first_row:after_row].set(solved)
    head_rows = jnp.tril(matrix[:2 * NB, :])
    matrix = matrix.at[:2 * NB, :].set(head_rows)
    return matrix.reshape(TRD, N_ROW * NB, TCD, N_COL * NB)
```

```python
import functools

import jax
import jax.numpy as jnp
from jax import lax
from jax.experimental import pallas as pl
from jax.experimental.pallas import tpu as pltpu
from jax.sharding import PartitionSpec as P

HIGHEST = lax.Precision.HIGHEST
LANE = 128
SUB = 8
X, Y, Z, CORE = 4, 8, 8, 2
N_ROW, N_COL = X * Y, Z * CORE
NB = 256
BOTH = ("row", "col")


def device(x, y, z, core):
    return (x * Y + y) * N_COL + z * CORE + core


def dot_nt(a, b):
    return lax.dot_general(a, b, (((1,), (1,)), ((), ())), precision=HIGHEST, preferred_element_type=jnp.float32)


def dot_nn(a, b):
    return lax.dot_general(a, b, (((1,), (0,)), ((), ())), precision=HIGHEST, preferred_element_type=jnp.float32)


def factor_block(rows):
    count = len(rows)
    rows = list(rows)
    sub = lax.broadcasted_iota(jnp.int32, (SUB, LANE), 0)
    lane = lax.broadcasted_iota(jnp.int32, (SUB, LANE), 1)
    aug = [jnp.where(lane == sub + SUB * g, 1.0, 0.0).astype(jnp.float32) for g in range(count)]
    for p in range(count):
        cols = [
            [jnp.broadcast_to(rows[g][:, SUB * p + k : SUB * p + k + 1], (SUB, LANE)) for g in range(p, count)]
            for k in range(SUB)
        ]
        r, e = rows[p], aug[p]
        xs, ys = [], []
        for k in range(SUB):
            scale = lax.rsqrt(jnp.broadcast_to(cols[k][0][k : k + 1, :], (SUB, LANE)))
            ck = [c * scale for c in cols[k]]
            cols[k] = ck
            x = jnp.broadcast_to(r[k : k + 1, :], (SUB, LANE)) * scale
            y = jnp.broadcast_to(e[k : k + 1, :], (SUB, LANE)) * scale
            xs.append(x)
            ys.append(y)
            if k < SUB - 1:
                below = jnp.where(sub > k, ck[0], 0.0)
                r = r - below * x
                e = e - below * y
                for m in range(k + 1, SUB):
                    s = jnp.broadcast_to(ck[0][m : m + 1, :], (SUB, LANE))
                    cols[m] = [c - d * s for c, d in zip(cols[m], ck)]
        for i, g in enumerate(range(p + 1, count)):
            a, b = rows[g], aug[g]
            for k in range(SUB):
                a = a - cols[k][i + 1] * xs[k]
                b = b - cols[k][i + 1] * ys[k]
            rows[g], aug[g] = a, b
        x, y = xs[0], ys[0]
        for k in range(1, SUB):
            x = jnp.where(sub == k, xs[k], x)
            y = jnp.where(sub == k, ys[k], y)
        rows[p] = jnp.where(lane >= sub + SUB * p, x, 0.0)
        aug[p] = y
    return rows, aug


def factor_kernel(d00_ref, d10_ref, d11_ref, l_ref, w_ref, a_ref):
    n = a_ref.shape[0]
    half = n // 2
    a_ref[:half, :half] = d00_ref[...]
    a_ref[half:, :half] = d10_ref[...]
    a_ref[:half, half:] = jnp.zeros((half, half), jnp.float32)
    a_ref[half:, half:] = d11_ref[...]
    l_ref[...] = jnp.zeros_like(l_ref)
    w_ref[...] = jnp.zeros_like(w_ref)

    def step(b, carry):
        o = pl.multiple_of(b * LANE, LANE)
        blk = pl.ds(o, LANE)
        rows = [a_ref[pl.ds(pl.multiple_of(o + SUB * g, SUB), SUB), blk] for g in range(LANE // SUB)]
        up, inv = factor_block(rows)
        up, inv = jnp.concatenate(up, 0), jnp.concatenate(inv, 0)
        below = lax.broadcasted_iota(jnp.int32, (n, LANE), 0) >= o + LANE
        panel = jnp.where(below, dot_nt(a_ref[:, blk], inv), 0.0)
        a_ref[...] = a_ref[...] - dot_nt(panel, panel)
        rest = dot_nn(l_ref[blk, :], w_ref[...])
        w_ref[blk, :] = -dot_nn(inv, rest)
        w_ref[blk, blk] = inv
        l_ref[:, blk] = panel
        l_ref[blk, blk] = up.T
        return carry

    lax.fori_loop(0, n // LANE, step, 0)


def factor(d00, d10, d11):
    n = 2 * NB
    return pl.pallas_call(
        factor_kernel,
        out_shape=[jax.ShapeDtypeStruct((n, n), jnp.float32)] * 2,
        in_specs=[pl.BlockSpec(memory_space=pltpu.VMEM)] * 3,
        out_specs=[pl.BlockSpec(memory_space=pltpu.VMEM)] * 2,
        scratch_shapes=[pltpu.VMEM((n, n), jnp.float32)],
        compiler_params=pltpu.CompilerParams(vmem_limit_bytes=32 * 2**20),
        name="factor",
    )(d00, d10, d11)


def split(x):
    hi = x.astype(jnp.bfloat16)
    return hi, (x - hi.astype(jnp.float32)).astype(jnp.bfloat16)


def dot3(a, b):
    def dot(u, v):
        return lax.dot_general(u, v, (((1,), (1,)), ((), ())), preferred_element_type=jnp.float32)

    return dot(a[0], b[0]) + (dot(a[0], b[1]) + dot(a[1], b[0]))


def solve(p0, p1, w):
    w00 = split(w[:NB, :NB])
    w10 = split(w[NB:, :NB])
    w11 = split(w[NB:, NB:])
    p0, p1 = split(p0), split(p1)
    return dot3(p0, w00), dot3(p0, w10) + dot3(p1, w11)


def update_kernel(rc_ref, cov_ref, r0_ref, r1_ref, g_ref, w_ref, l_ref, out_ref, hi_ref, lo_ref):
    step = pl.program_id(0)
    rows = cov_ref.shape[1]
    tcd = cov_ref.shape[2]

    @pl.when(step == 0)
    def _():
        w = w_ref[...]
        for b in range(tcd):
            p0 = g_ref[2 * (b % 2), :, b // 2].reshape(NB, NB)
            p1 = g_ref[2 * (b % 2) + 1, :, b // 2].reshape(NB, NB)
            for k, s in enumerate(solve(p0, p1, w)):
                hi, lo = split(s)
                hi_ref[b, :, k * NB : (k + 1) * NB] = hi
                lo_ref[b, :, k * NB : (k + 1) * NB] = lo

    s0, s1 = solve(r0_ref[0], r1_ref[0], w_ref[...])
    left = split(jnp.concatenate([s0, s1], 1))
    for b in range(tcd):
        out_ref[0, :, b, :] = cov_ref[0, :, b, :] - dot3(left, (hi_ref[b], lo_ref[b]))
    row, col = rc_ref[0], rc_ref[1]
    per_tile = NB // rows
    tile_row = row + N_ROW * (step // per_tile)

    @pl.when(jnp.logical_and(tile_row >= 2, col == 0))
    def _():
        out_ref[0, :, 0, :] = s0

    @pl.when(jnp.logical_and(tile_row >= 2, col == 1))
    def _():
        out_ref[0, :, 0, :] = s1

    @pl.when(tile_row < 2)
    def _():
        out_ref[...] = jnp.zeros_like(out_ref)

    @pl.when(jnp.logical_and(tile_row < 2, col < 2))
    def _():
        first = pl.multiple_of(tile_row * NB + lax.rem(step, per_tile) * rows, rows)
        out_ref[0, :, 0, :] = l_ref[pl.ds(first, rows), pl.ds(pl.multiple_of(col * NB, NB), NB)]


def update(cov, r0, r1, g, w, lower):
    trd, nb, tcd, _ = cov.shape
    rows = 128
    per_tile = nb // rows
    rc = jnp.stack([lax.axis_index("row"), lax.axis_index("col")]).astype(jnp.int32)
    whole = pl.BlockSpec(memory_space=pltpu.VMEM)
    block = pl.BlockSpec((1, rows, tcd, nb), lambda s: (s // per_tile, s % per_tile, 0, 0))
    piece = pl.BlockSpec((1, rows, nb), lambda s: (s // per_tile, s % per_tile, 0))
    return pl.pallas_call(
        update_kernel,
        grid=(trd * per_tile,),
        out_shape=jax.ShapeDtypeStruct(cov.shape, jnp.float32),
        in_specs=[pl.BlockSpec(memory_space=pltpu.SMEM), block, piece, piece, whole, whole, whole],
        out_specs=block,
        scratch_shapes=[pltpu.VMEM((tcd, nb, 2 * nb), jnp.bfloat16)] * 2,
        compiler_params=pltpu.CompilerParams(vmem_limit_bytes=48 * 2**20),
        name="update",
    )(rc, cov, r0, r1, g, w, lower)


def spread_diagonal(panel, x, y, z, core):
    tile = panel[0].reshape(X, NB // X, NB)
    roots = ((0, 0), (1, 0), (1, 1))
    piece = jnp.where(x == 0, tile[0], 0.0)
    for s in range(1, X):
        pairs = [(device(0, j, 0, c), device(s, j, 0, c)) for j, c in roots]
        piece = piece + lax.ppermute(tile[s], BOTH, pairs)
    first = jnp.where(y == 0, piece, 0.0)
    second = jnp.where(y == 1, piece, 0.0)
    for s in range(1, Y):
        pairs = [(device(i, j, 0, c), device(i, (j + s) % Y, 0, c)) for i in range(X) for j, c in roots]
        came = lax.ppermute(piece, BOTH, pairs)
        first = first + jnp.where(y == s, came, 0.0)
        second = second + jnp.where(y == (s + 1) % Y, came, 0.0)
    here = jnp.where(z == 0, jnp.stack([first, second]), 0.0)
    mine = here
    for s in range(1, Z):
        pairs = [(device(i, j, 0, c), device(i, j, s, c)) for i in range(X) for j in range(Y) for c in range(CORE)]
        mine = mine + lax.ppermute(here, BOTH, pairs)
    groups = [[i * Y + j for i in range(X)] for j in range(Y)]
    mine = lax.all_to_all(jnp.broadcast_to(mine[None], (X,) + mine.shape), "row", 0, 0, axis_index_groups=groups)
    mine = jnp.moveaxis(mine, 0, 1).reshape(2, NB, NB)
    other = lax.ppermute(mine, "col", [(i, i ^ 1) for i in range(N_COL)])
    d00 = jnp.where(core == 0, mine[0], other[0])
    d10 = jnp.where(core == 0, mine[1], other[1])
    d11 = jnp.where(core == 0, other[1], mine[1])
    return d00, d10, d11


def column_panels(panel, x, y):
    parts = panel.reshape(2, Y, NB // Y, NB)
    mine = None
    for s in range(Y):
        pairs = [
            (p * N_COL + k, device(2 * (p // N_COL) + k, s, (p % N_COL) // CORE, p % CORE))
            for p in range(N_ROW)
            for k in range(2)
        ]
        came = lax.ppermute(parts[:, s], BOTH, pairs)
        mine = came if mine is None else mine + came
    groups = [[i * Y + j for j in range(Y)] for i in range(X)]
    mine = lax.all_to_all(jnp.broadcast_to(mine[None], (Y,) + mine.shape), "row", 0, 0, axis_index_groups=groups)
    groups = [[i * Y + j for i in range(X)] for j in range(Y)]
    return lax.all_gather(mine, "row", axis_index_groups=groups)


def row_panels(panel, core):
    groups = [[2 * i + k for i in range(Z)] for k in range(CORE)]
    mine = lax.all_gather(panel, "col", axis_index_groups=groups)[0]
    other = lax.ppermute(mine, "col", [(i, i ^ 1) for i in range(N_COL)])
    return jnp.where(core == 0, mine, other), jnp.where(core == 0, other, mine)


def on_device(cov):
    row, col = lax.axis_index("row"), lax.axis_index("col")
    x, y, z, core = row // Y, row % Y, col // CORE, col % CORE
    panel = cov[:, :, 0, :]
    r0, r1 = row_panels(panel, core)
    g = column_panels(panel, x, y)
    d00, d10, d11 = spread_diagonal(panel, x, y, z, core)
    lower, w = factor(d00, d10, d11)
    return update(cov, r0, r1, g, w, lower)


def solution(mesh):
    placed = (P(None, "row", None, "col"),)
    return jax.shard_map(
        on_device,
        mesh=mesh,
        in_specs=placed,
        out_specs=P(None, "row", None, "col"),
        check_vma=False,
    )
```

```python
import jax
import jax.numpy as jnp
from jax import lax
from jax.experimental import pallas as pl
from jax.experimental.pallas import tpu as pltpu
from jax.sharding import PartitionSpec as P

LANE = 128
SUB = 8
X, Y, Z, CORE = 4, 8, 8, 2
N_ROW, N_COL = X * Y, Z * CORE
NB = 256
PART = NB // Z
BOTH = ("row", "col")
ROOTS = ((0, 0), (1, 0), (1, 1))


def device(x, y, z, core):
    return (x * Y + y) * N_COL + z * CORE + core


def dot_nt(a, b):
    return lax.dot_general(
        a, b, (((1,), (1,)), ((), ())), precision=lax.Precision.HIGHEST, preferred_element_type=jnp.float32
    )


def dot_nn(a, b):
    return lax.dot_general(
        a, b, (((1,), (0,)), ((), ())), precision=lax.Precision.HIGHEST, preferred_element_type=jnp.float32
    )


def column(rows, k):
    return jnp.broadcast_to(rows[:, k : k + 1], (SUB, LANE))


def total(terms):
    terms = list(terms)
    while len(terms) > 1:
        terms = [sum(terms[i : i + 2]) for i in range(0, len(terms), 2)]
    return terms[0]


def factor_block(rows, s_ref):
    count = len(rows)
    rows = list(rows)
    sub = lax.broadcasted_iota(jnp.int32, (SUB, LANE), 0)
    lane = lax.broadcasted_iota(jnp.int32, (SUB, LANE), 1)
    aug = [jnp.where(lane == sub + SUB * g, 1.0, 0.0).astype(jnp.float32) for g in range(count)]
    span = SUB * (SUB + 2)
    for p in range(count):
        base = (p % 2) * span
        for k in range(SUB):
            s_ref[base + SUB * k : base + SUB * (k + 1), :] = column(rows[p], SUB * p + k)
        s_ref[base + SUB * SUB : base + SUB * (SUB + 1), :] = rows[p]
        s_ref[base + SUB * (SUB + 1) : base + span, :] = aug[p]

        def spread(i, base=base):
            return jnp.broadcast_to(s_ref[base + i : base + i + 1, :], (SUB, LANE))

        a = {(m, k): spread(SUB * k + m) for k in range(SUB) for m in range(k, SUB)}
        low, scale = {}, []
        for k in range(0, SUB, 2):
            first, cross, second = a[k, k], a[k + 1, k], a[k + 1, k + 1]
            r1 = lax.rsqrt(first)
            r2 = lax.rsqrt(first * second - cross * cross) * (first * r1)
            scale += [r1, r2]
            low[k + 1, k] = cross * r1
            for m in range(k + 2, SUB):
                low[m, k] = a[m, k] * r1
                low[m, k + 1] = (a[m, k + 1] - low[m, k] * low[k + 1, k]) * r2
            for m in range(k + 2, SUB):
                for n in range(k + 2, m + 1):
                    a[m, n] = a[m, n] - (low[m, k] * low[n, k] + low[m, k + 1] * low[n, k + 1])
        xs, ys = [], []
        for k in range(SUB):
            x, y = spread(SUB * SUB + k), spread(SUB * (SUB + 1) + k)
            for j in range(k):
                x = x - low[k, j] * xs[j]
                y = y - low[k, j] * ys[j]
            xs.append(x * scale[k])
            ys.append(y * scale[k])
        for g in range(p + 1, count):
            left = []
            for k in range(SUB):
                t = column(rows[g], SUB * p + k)
                for j in range(k):
                    t = t - left[j] * low[k, j]
                left.append(t * scale[k])
            rows[g] = rows[g] - total(c * x for c, x in zip(left, xs))
            aug[g] = aug[g] - total(c * y for c, y in zip(left, ys))
        x, y = xs[0], ys[0]
        for k in range(1, SUB):
            x = jnp.where(sub == k, xs[k], x)
            y = jnp.where(sub == k, ys[k], y)
        rows[p] = jnp.where(lane >= sub + SUB * p, x, 0.0)
        aug[p] = y
    return jnp.concatenate(rows, 0), jnp.concatenate(aug, 0)


def factor_kernel(core_ref, mine_ref, other_ref, l_ref, w_ref, a_ref, s_ref):
    n = a_ref.shape[0]
    nb = n // LANE

    for core, (first, second) in enumerate(((mine_ref, other_ref), (other_ref, mine_ref))):

        @pl.when(core_ref[0] == core)
        def _():
            a_ref[:NB, :NB] = first[:, 0].reshape(NB, NB)
            a_ref[NB:, :NB] = first[:, 1].reshape(NB, NB)
            a_ref[NB:, NB:] = second[:, 1].reshape(NB, NB)

    def blk(i):
        return slice(i * LANE, (i + 1) * LANE)

    inverses = []
    for b in range(nb):
        rows = [a_ref[b * LANE + SUB * g : b * LANE + SUB * (g + 1), blk(b)] for g in range(LANE // SUB)]
        upper, inverse = factor_block(rows, s_ref)
        inverses.append(inverse)
        l_ref[blk(b), blk(b)] = upper
        for i in range(b + 1, nb):
            panel = dot_nt(a_ref[blk(i), blk(b)], inverse)
            l_ref[blk(i), blk(b)] = panel
            for j in range(b + 1, i + 1):
                a_ref[blk(i), blk(j)] = a_ref[blk(i), blk(j)] - dot_nt(panel, l_ref[blk(j), blk(b)])
        half, odd = divmod(b, 2)
        w_ref[half, blk(odd), blk(odd)] = inverse
        if odd:
            w_ref[half, blk(0), blk(1)] = jnp.zeros((LANE, LANE), jnp.float32)
            w_ref[half, blk(1), blk(0)] = -dot_nn(inverse, dot_nn(l_ref[blk(b), blk(b - 1)], inverses[b - 1]))


def factor(core, mine, other):
    n = 2 * NB
    vmem = pl.BlockSpec(memory_space=pltpu.VMEM)
    return pl.pallas_call(
        factor_kernel,
        out_shape=[jax.ShapeDtypeStruct((n, n), jnp.float32), jax.ShapeDtypeStruct((2, NB, NB), jnp.float32)],
        in_specs=[pl.BlockSpec(memory_space=pltpu.SMEM), vmem, vmem],
        out_specs=[vmem, vmem],
        scratch_shapes=[pltpu.VMEM((n, n), jnp.float32), pltpu.VMEM((2 * SUB * (SUB + 2), LANE), jnp.float32)],
        compiler_params=pltpu.CompilerParams(vmem_limit_bytes=16 * 2**20),
        name="factor",
    )(core, mine, other)


def split(x):
    hi = x.astype(jnp.bfloat16)
    rest = x - hi.astype(jnp.float32)
    mid = rest.astype(jnp.bfloat16)
    return hi, mid, (rest - mid.astype(jnp.float32)).astype(jnp.bfloat16)


def dot6(a, b):
    out = None
    for i in range(3):
        for j in range(3 - i):
            t = lax.dot_general(a[i], b[j], (((1,), (1,)), ((), ())), preferred_element_type=jnp.float32)
            out = t if out is None else out + t
    return out


def update_kernel(place_ref, cov_hbm, r_ref, g_ref, w_ref, l_ref, out_ref, cov_ref, s_ref, sem):
    trd, nb, tcd, _ = cov_ref.shape
    copy = pltpu.make_async_copy(cov_hbm, cov_ref, sem)
    copy.start()
    w0, l10, w1 = split(w_ref[0]), split(l_ref[NB:, :NB]), split(w_ref[1])

    def solve(p0, p1):
        s0 = dot6(split(p0), w0)
        a0 = split(s0)
        s1 = dot6(split(p1 - dot6(a0, l10)), w1)
        return s0, a0, s1, split(s1)

    for b in range(0, tcd, 2):
        p0, p1 = (
            jnp.concatenate([g_ref[2 * h + k, :, b // 2].reshape(NB, NB) for h in range(2)], 0) for k in range(2)
        )
        _, a0, _, a1 = solve(p0, p1)
        for j in range(3):
            for h in range(2):
                s_ref[j, b + h, :, :NB] = a0[j][h * NB : (h + 1) * NB]
                s_ref[j, b + h, :, NB:] = a1[j][h * NB : (h + 1) * NB]
    p0, p1 = (jnp.concatenate([r_ref[:, k, a].reshape(NB, NB) for a in range(trd)], 0) for k in range(2))
    s0, a0, s1, a1 = solve(p0, p1)
    left = [jnp.concatenate([u, v], 1) for u, v in zip(a0, a1)]
    copy.wait()
    for b in range(tcd):
        u = dot6(left, [s_ref[j, b] for j in range(3)])
        for a in range(trd):
            out_ref[a, :, b, :] = cov_ref[a, :, b, :] - u[a * nb : (a + 1) * nb]
    row, col = place_ref[0], place_ref[1]
    for k, s in enumerate((s0, s1)):

        @pl.when(col == k)
        def _():
            for a in range(trd):
                out_ref[a, :, 0, :] = s[a * nb : (a + 1) * nb]

    @pl.when(row < 2)
    def _():
        out_ref[0] = jnp.zeros_like(out_ref[0])

    for i in range(2):
        for j in range(i + 1):

            @pl.when(jnp.logical_and(row == i, col == j))
            def _():
                for u in range(2):
                    for v in range(2):
                        if i == j and u < v:
                            continue
                        block = l_ref[
                            i * NB + u * LANE : i * NB + (u + 1) * LANE, j * NB + v * LANE : j * NB + (v + 1) * LANE
                        ]
                        out_ref[0, u * LANE : (u + 1) * LANE, 0, v * LANE : (v + 1) * LANE] = (
                            block.T if i == j and u == v else block
                        )


def update(place, cov, r, g, w, lower):
    trd, nb, tcd, _ = cov.shape
    vmem = pl.BlockSpec(memory_space=pltpu.VMEM)
    return pl.pallas_call(
        update_kernel,
        out_shape=jax.ShapeDtypeStruct(cov.shape, jnp.float32),
        in_specs=[pl.BlockSpec(memory_space=pltpu.SMEM), pl.BlockSpec(memory_space=pl.ANY), vmem, vmem, vmem, vmem],
        out_specs=vmem,
        scratch_shapes=[
            pltpu.VMEM(cov.shape, jnp.float32),
            pltpu.VMEM((3, tcd, nb, 2 * nb), jnp.bfloat16),
            pltpu.SemaphoreType.DMA,
        ],
        compiler_params=pltpu.CompilerParams(vmem_limit_bytes=28 * 2**20),
        name="update",
    )(place, cov, r.reshape(Z, CORE, trd, PART, nb), g, w, lower)


def shared(block, groups):
    many = jnp.broadcast_to(block[None], (len(groups[0]),) + block.shape)
    return lax.all_to_all(many, "row", 0, 0, axis_index_groups=groups)


def on_device(cov):
    row, col = lax.axis_index("row"), lax.axis_index("col")
    x, z, core = row // Y, col // CORE, col % CORE
    panel = cov[:, :, 0, :].reshape(2, Z, PART, NB)

    mine = jnp.where(z == 0, panel[:, 0], 0.0)
    for s in range(1, Z):
        pairs = [(p * N_COL + k, p * N_COL + s * CORE + k) for p in range(N_ROW) for k in range(CORE)]
        mine = mine + lax.ppermute(panel[:, s], BOTH, pairs)
    r = lax.all_gather(mine, "col")

    head = jnp.where(x == 0, mine[0], 0.0)
    for s in range(1, X):
        pairs = [(device(0, y, c, k), device(s, y, c, k)) for c in range(Z) for y, k in ROOTS]
        head = head + lax.ppermute(mine[0], BOTH, pairs)

    pairs = [
        (p * N_COL + c * CORE + k, device(2 * (p // N_COL) + k, c, (p % N_COL) // CORE, p % CORE))
        for p in range(N_ROW)
        for c in range(Z)
        for k in range(CORE)
    ]
    mine = lax.ppermute(mine, BOTH, pairs)
    got = shared(jnp.concatenate([mine, head[None]]), [[i * Y + j for j in range(Y)] for i in range(X)])
    g = lax.all_gather(got[:, :2], "row", axis_index_groups=[[i * Y + j for i in range(X)] for j in range(Y)])

    many = jnp.broadcast_to(got[None, :2, 2], (Z, 2, PART, NB))
    tiles = lax.all_to_all(many, "col", 0, 0, axis_index_groups=[[c * CORE + k for c in range(Z)] for k in range(CORE)])
    other = lax.ppermute(tiles, "col", [(i, i ^ 1) for i in range(N_COL)])
    lower, w = factor(core.astype(jnp.int32).reshape(1), tiles, other)
    return update(jnp.stack([row, col]).astype(jnp.int32), cov, r, g, w, lower)


def solution(mesh):
    placed = (P(None, "row", None, "col"),)
    return jax.shard_map(
        on_device,
        mesh=mesh,
        in_specs=placed,
        out_specs=P(None, "row", None, "col"),
        check_vma=False,
    )
```

```python
import jax
import jax.numpy as jnp
from jax import lax
from jax.experimental import pallas as pl
from jax.experimental.pallas import tpu as pltpu
from jax.sharding import PartitionSpec as P

LANE = 128
SUB = 8
X, Y, Z, CORE = 4, 8, 8, 2
N_ROW, N_COL = X * Y, Z * CORE
NB = 256
PART = NB // Z
BOTH = ("row", "col")
ROOTS = ((0, 0), (1, 0), (1, 1))


def device(x, y, z, core):
    return (x * Y + y) * N_COL + z * CORE + core


def dot_nt(a, b):
    return lax.dot_general(
        a, b, (((1,), (1,)), ((), ())), precision=lax.Precision.HIGHEST, preferred_element_type=jnp.float32
    )


def dot_nn(a, b):
    return lax.dot_general(
        a, b, (((1,), (0,)), ((), ())), precision=lax.Precision.HIGHEST, preferred_element_type=jnp.float32
    )


def column(rows, k):
    return jnp.broadcast_to(rows[:, k : k + 1], (SUB, LANE))


def total(terms):
    terms = list(terms)
    while len(terms) > 1:
        terms = [sum(terms[i : i + 2]) for i in range(0, len(terms), 2)]
    return terms[0]


def factor_block(rows, s_ref):
    count = len(rows)
    rows = list(rows)
    sub = lax.broadcasted_iota(jnp.int32, (SUB, LANE), 0)
    lane = lax.broadcasted_iota(jnp.int32, (SUB, LANE), 1)
    aug = [jnp.where(lane == sub + SUB * g, 1.0, 0.0).astype(jnp.float32) for g in range(count)]
    span = SUB * (SUB + 2)
    for p in range(count):
        base = (p % 2) * span
        for k in range(SUB):
            s_ref[base + SUB * k : base + SUB * (k + 1), :] = column(rows[p], SUB * p + k)
        s_ref[base + SUB * SUB : base + SUB * (SUB + 1), :] = rows[p]
        s_ref[base + SUB * (SUB + 1) : base + span, :] = aug[p]

        def spread(i, base=base):
            return jnp.broadcast_to(s_ref[base + i : base + i + 1, :], (SUB, LANE))

        a = {(m, k): spread(SUB * k + m) for k in range(SUB) for m in range(k, SUB)}
        low, scale = {}, []
        for k in range(0, SUB, 2):
            first, cross, second = a[k, k], a[k + 1, k], a[k + 1, k + 1]
            r1 = lax.rsqrt(first)
            r2 = lax.rsqrt(first * second - cross * cross) * (first * r1)
            scale += [r1, r2]
            low[k + 1, k] = cross * r1
            for m in range(k + 2, SUB):
                low[m, k] = a[m, k] * r1
                low[m, k + 1] = (a[m, k + 1] - low[m, k] * low[k + 1, k]) * r2
            for m in range(k + 2, SUB):
                for n in range(k + 2, m + 1):
                    a[m, n] = a[m, n] - (low[m, k] * low[n, k] + low[m, k + 1] * low[n, k + 1])
        xs, ys = [], []
        for k in range(SUB):
            x, y = spread(SUB * SUB + k), spread(SUB * (SUB + 1) + k)
            for j in range(k):
                x = x - low[k, j] * xs[j]
                y = y - low[k, j] * ys[j]
            xs.append(x * scale[k])
            ys.append(y * scale[k])
        for g in range(p + 1, count):
            left = []
            for k in range(SUB):
                t = column(rows[g], SUB * p + k)
                for j in range(k):
                    t = t - left[j] * low[k, j]
                left.append(t * scale[k])
            rows[g] = rows[g] - total(c * x for c, x in zip(left, xs))
            aug[g] = aug[g] - total(c * y for c, y in zip(left, ys))
        x, y = xs[0], ys[0]
        for k in range(1, SUB):
            x = jnp.where(sub == k, xs[k], x)
            y = jnp.where(sub == k, ys[k], y)
        rows[p] = jnp.where(lane >= sub + SUB * p, x, 0.0)
        aug[p] = y
    return jnp.concatenate(rows, 0), jnp.concatenate(aug, 0)


def split(x):
    hi = x.astype(jnp.bfloat16)
    rest = x - hi.astype(jnp.float32)
    mid = rest.astype(jnp.bfloat16)
    return hi, mid, (rest - mid.astype(jnp.float32)).astype(jnp.bfloat16)


def dot6(a, b):
    out = None
    for i in range(3):
        for j in range(3 - i):
            t = lax.dot_general(a[i], b[j], (((1,), (1,)), ((), ())), preferred_element_type=jnp.float32)
            out = t if out is None else out + t
    return out


def solve(p0, p1, w0, l10, w1):
    a0 = split(dot6(split(p0), w0))
    return a0, split(dot6(split(p1 - dot6(a0, l10)), w1))


def factor_kernel(tiles_ref, r_ref, l_ref, w_ref, s_ref, a_ref, v_ref, spread_ref):
    n = a_ref.shape[0]
    nb = n // LANE
    a_ref[:NB, :NB] = tiles_ref[:, 0].reshape(NB, NB)
    a_ref[NB:, :NB] = tiles_ref[:, 1].reshape(NB, NB)
    a_ref[NB:, NB:] = tiles_ref[:, 2].reshape(NB, NB)

    def blk(i):
        return slice(i * LANE, (i + 1) * LANE)

    inverses = []
    for b in range(nb):
        rows = [a_ref[b * LANE + SUB * g : b * LANE + SUB * (g + 1), blk(b)] for g in range(LANE // SUB)]
        upper, inverse = factor_block(rows, spread_ref)
        inverses.append(inverse)
        l_ref[blk(b), blk(b)] = upper
        for i in range(b + 1, nb):
            panel = dot_nt(a_ref[blk(i), blk(b)], inverse)
            l_ref[blk(i), blk(b)] = panel
            for j in range(b + 1, i + 1):
                a_ref[blk(i), blk(j)] = a_ref[blk(i), blk(j)] - dot_nt(panel, l_ref[blk(j), blk(b)])
        half, odd = divmod(b, 2)
        v_ref[half, blk(odd), blk(odd)] = inverse
        if odd:
            v_ref[half, blk(0), blk(1)] = jnp.zeros((LANE, LANE), jnp.float32)
            v_ref[half, blk(1), blk(0)] = -dot_nn(inverse, dot_nn(l_ref[blk(b), blk(b - 1)], inverses[b - 1]))
    weights = [split(m) for m in (v_ref[0], l_ref[NB:, :NB], v_ref[1])]
    for i, parts in enumerate(weights):
        for j, part in enumerate(parts):
            w_ref[i, j] = part
    trd = r_ref.shape[2]
    p0, p1 = (jnp.concatenate([r_ref[:, k, a].reshape(NB, NB) for a in range(trd)], 0) for k in range(2))
    for k, parts in enumerate(solve(p0, p1, *weights)):
        for j, part in enumerate(parts):
            s_ref[j, :, k * NB : (k + 1) * NB] = part


def factor(tiles, r):
    n = 2 * NB
    trd = r.shape[1]
    vmem = pl.BlockSpec(memory_space=pltpu.VMEM)
    return pl.pallas_call(
        factor_kernel,
        out_shape=[
            jax.ShapeDtypeStruct((n, n), jnp.float32),
            jax.ShapeDtypeStruct((3, 3, NB, NB), jnp.bfloat16),
            jax.ShapeDtypeStruct((3, trd * NB, n), jnp.bfloat16),
        ],
        in_specs=[vmem, vmem],
        out_specs=[vmem, vmem, vmem],
        scratch_shapes=[
            pltpu.VMEM((n, n), jnp.float32),
            pltpu.VMEM((2, NB, NB), jnp.float32),
            pltpu.VMEM((2 * SUB * (SUB + 2), LANE), jnp.float32),
        ],
        compiler_params=pltpu.CompilerParams(vmem_limit_bytes=20 * 2**20),
        name="factor",
    )(tiles, r.reshape(Z, CORE, trd, PART, NB))


def update_kernel(place_ref, cov_hbm, g_hbm, w_ref, l_ref, left_ref, out_ref, cov_ref, g_ref, s_ref, sems):
    trd, nb, tcd, _ = cov_ref.shape
    copies = [pltpu.make_async_copy(g_hbm.at[:, :, a], g_ref.at[a], sems.at[a]) for a in range(2)]
    copies.append(pltpu.make_async_copy(cov_hbm, cov_ref, sems.at[2]))
    for copy in copies:
        copy.start()
    weights = [[w_ref[i, j] for j in range(3)] for i in range(3)]
    for a in range(2):
        copies[a].wait()
        p0, p1 = (
            jnp.concatenate([g_ref[a, :, 2 * h + k].reshape(NB, NB) for h in range(2)], 0) for k in range(2)
        )
        for k, parts in enumerate(solve(p0, p1, *weights)):
            for j, part in enumerate(parts):
                for h in range(2):
                    s_ref[j, 2 * a + h, :, k * NB : (k + 1) * NB] = part[h * NB : (h + 1) * NB]
    left = [left_ref[j] for j in range(3)]
    copies[2].wait()
    for b in range(tcd):
        u = dot6(left, [s_ref[j, b] for j in range(3)])
        for a in range(trd):
            out_ref[a, :, b, :] = cov_ref[a, :, b, :] - u[a * nb : (a + 1) * nb]
    row, col = place_ref[0], place_ref[1]
    for k in range(2):

        @pl.when(col == k)
        def _():
            s = sum(left_ref[j, :, k * NB : (k + 1) * NB].astype(jnp.float32) for j in (2, 1, 0))
            for a in range(trd):
                out_ref[a, :, 0, :] = s[a * nb : (a + 1) * nb]

    @pl.when(row < 2)
    def _():
        out_ref[0] = jnp.zeros_like(out_ref[0])

    for i in range(2):
        for j in range(i + 1):

            @pl.when(jnp.logical_and(row == i, col == j))
            def _():
                for u in range(2):
                    for v in range(2):
                        if i == j and u < v:
                            continue
                        block = l_ref[
                            i * NB + u * LANE : i * NB + (u + 1) * LANE, j * NB + v * LANE : j * NB + (v + 1) * LANE
                        ]
                        out_ref[0, u * LANE : (u + 1) * LANE, 0, v * LANE : (v + 1) * LANE] = (
                            block.T if i == j and u == v else block
                        )


def update(place, cov, g, w, lower, left):
    trd, nb, tcd, _ = cov.shape
    vmem = pl.BlockSpec(memory_space=pltpu.VMEM)
    hbm = pl.BlockSpec(memory_space=pl.ANY)
    return pl.pallas_call(
        update_kernel,
        out_shape=jax.ShapeDtypeStruct(cov.shape, jnp.float32),
        in_specs=[pl.BlockSpec(memory_space=pltpu.SMEM), hbm, hbm, vmem, vmem, vmem],
        out_specs=vmem,
        scratch_shapes=[
            pltpu.VMEM(cov.shape, jnp.float32),
            pltpu.VMEM((2, Y, X, PART, NB), jnp.float32),
            pltpu.VMEM((3, tcd, nb, 2 * nb), jnp.bfloat16),
            pltpu.SemaphoreType.DMA((3,)),
        ],
        compiler_params=pltpu.CompilerParams(vmem_limit_bytes=24 * 2**20),
        name="update",
    )(place, cov, g, w, lower, left)


def shared(block, axis, groups):
    many = jnp.broadcast_to(block[None], (len(groups[0]),) + block.shape)
    return lax.all_to_all(many, axis, 0, 0, axis_index_groups=groups)


def on_device(cov):
    row, col = lax.axis_index("row"), lax.axis_index("col")
    y, z = row % Y, col // CORE
    along_x = [[i * Y + j for i in range(X)] for j in range(Y)]
    along_y = [[i * Y + j for j in range(Y)] for i in range(X)]
    along_z = [[c * CORE + k for c in range(Z)] for k in range(CORE)]
    chips = [[c * CORE + k for k in range(CORE)] for c in range(Z)]
    panel = cov[:, :, 0, :].reshape(2, Z, PART, NB)

    mine = jnp.where(z == 0, panel[:, 0], 0.0)
    for s in range(1, Z):
        pairs = [(p * N_COL + k, p * N_COL + s * CORE + k) for p in range(N_ROW) for k in range(CORE)]
        mine = mine + lax.ppermute(panel[:, s], BOTH, pairs)
    r = lax.all_gather(mine, "col")

    pairs = [
        (p * N_COL + c * CORE + k, device(2 * (p // N_COL) + k, c, (p % N_COL) // CORE, p % CORE))
        for p in range(N_ROW)
        for c in range(Z)
        for k in range(CORE)
    ]
    moved = lax.ppermute(mine, BOTH, pairs)

    first = jnp.where(y == 0, mine[0], 0.0)
    second = jnp.where(y == 1, mine[0], 0.0)
    for s in range(1, Y):
        pairs = [(device(0, j, c, k), device(0, (j + s) % Y, c, k)) for c in range(Z) for j, k in ROOTS]
        came = lax.ppermute(mine[0], BOTH, pairs)
        first = jnp.where(y == s, came, first)
        second = jnp.where(y == (s + 1) % Y, came, second)
    got = shared(jnp.concatenate([moved, first[None], second[None]]), "row", along_x)
    g = lax.all_gather(got[:, :2], "row", axis_index_groups=along_y)

    head = lax.all_gather(got[0, 2:], "col", axis_index_groups=chips)
    tiles = shared(jnp.stack([head[0, 0], head[0, 1], head[1, 1]]), "col", along_z)
    lower, w, left = factor(tiles, r)
    return update(jnp.stack([row, col]).astype(jnp.int32), cov, g, w, lower, left)


def solution(mesh):
    placed = (P(None, "row", None, "col"),)
    return jax.shard_map(
        on_device,
        mesh=mesh,
        in_specs=placed,
        out_specs=P(None, "row", None, "col"),
        check_vma=False,
    )
```

```python
import jax
import jax.numpy as jnp
from jax import lax
from jax.experimental import pallas as pl
from jax.experimental.pallas import tpu as pltpu
from jax.sharding import PartitionSpec as P

LANE = 128
SUB = 8
X, Y, Z, CORE = 4, 8, 8, 2
N_ROW, N_COL = X * Y, Z * CORE
NB = 256
PART = NB // Z
BOTH = ("row", "col")
ROOTS = ((0, 0), (1, 0), (1, 1))


def device(x, y, z, core):
    return (x * Y + y) * N_COL + z * CORE + core


def dot_nt(a, b):
    return lax.dot_general(
        a, b, (((1,), (1,)), ((), ())), precision=lax.Precision.HIGHEST, preferred_element_type=jnp.float32
    )


def dot_nn(a, b):
    return lax.dot_general(
        a, b, (((1,), (0,)), ((), ())), precision=lax.Precision.HIGHEST, preferred_element_type=jnp.float32
    )


def column(rows, k):
    return jnp.broadcast_to(rows[:, k : k + 1], (SUB, LANE))


def total(terms):
    terms = list(terms)
    while len(terms) > 1:
        terms = [sum(terms[i : i + 2]) for i in range(0, len(terms), 2)]
    return terms[0]


def factor_block(rows, s_ref):
    count = len(rows)
    rows = list(rows)
    sub = lax.broadcasted_iota(jnp.int32, (SUB, LANE), 0)
    lane = lax.broadcasted_iota(jnp.int32, (SUB, LANE), 1)
    aug = [jnp.where(lane == sub + SUB * g, 1.0, 0.0).astype(jnp.float32) for g in range(count)]
    span = SUB * (SUB + 2)
    for p in range(count):
        base = (p % 2) * span
        for k in range(SUB):
            s_ref[base + SUB * k : base + SUB * (k + 1), :] = column(rows[p], SUB * p + k)
        s_ref[base + SUB * SUB : base + SUB * (SUB + 1), :] = rows[p]
        s_ref[base + SUB * (SUB + 1) : base + span, :] = aug[p]

        def spread(i, base=base):
            return jnp.broadcast_to(s_ref[base + i : base + i + 1, :], (SUB, LANE))

        a = {(m, k): spread(SUB * k + m) for k in range(SUB) for m in range(k, SUB)}
        low, scale = {}, []
        for k in range(0, SUB, 2):
            first, cross, second = a[k, k], a[k + 1, k], a[k + 1, k + 1]
            r1 = lax.rsqrt(first)
            r2 = lax.rsqrt(first * second - cross * cross) * (first * r1)
            scale += [r1, r2]
            low[k + 1, k] = cross * r1
            for m in range(k + 2, SUB):
                low[m, k] = a[m, k] * r1
                low[m, k + 1] = (a[m, k + 1] - low[m, k] * low[k + 1, k]) * r2
            for m in range(k + 2, SUB):
                for n in range(k + 2, m + 1):
                    a[m, n] = a[m, n] - (low[m, k] * low[n, k] + low[m, k + 1] * low[n, k + 1])
        xs, ys = [], []
        for k in range(SUB):
            x, y = spread(SUB * SUB + k), spread(SUB * (SUB + 1) + k)
            for j in range(k):
                x = x - low[k, j] * xs[j]
                y = y - low[k, j] * ys[j]
            xs.append(x * scale[k])
            ys.append(y * scale[k])
        for g in range(p + 1, count):
            left = []
            for k in range(SUB):
                t = column(rows[g], SUB * p + k)
                for j in range(k):
                    t = t - left[j] * low[k, j]
                left.append(t * scale[k])
            rows[g] = rows[g] - total(c * x for c, x in zip(left, xs))
            aug[g] = aug[g] - total(c * y for c, y in zip(left, ys))
        x, y = xs[0], ys[0]
        for k in range(1, SUB):
            x = jnp.where(sub == k, xs[k], x)
            y = jnp.where(sub == k, ys[k], y)
        rows[p] = jnp.where(lane >= sub + SUB * p, x, 0.0)
        aug[p] = y
    return jnp.concatenate(rows, 0), jnp.concatenate(aug, 0)


def split(x):
    hi = x.astype(jnp.bfloat16)
    rest = x - hi.astype(jnp.float32)
    mid = rest.astype(jnp.bfloat16)
    return hi, mid, (rest - mid.astype(jnp.float32)).astype(jnp.bfloat16)


def dot6(a, b):
    out = None
    for i in range(3):
        for j in range(3 - i):
            t = lax.dot_general(a[i], b[j], (((1,), (1,)), ((), ())), preferred_element_type=jnp.float32)
            out = t if out is None else out + t
    return out


def solve(p0, p1, w0, l10, w1):
    a0 = split(dot6(split(p0), w0))
    return a0, split(dot6(split(p1 - dot6(a0, l10)), w1))


def factor_kernel(tiles_ref, r_hbm, l_hbm, w_hbm, s_hbm, a_ref, l_ref, w_ref, r_ref, s_ref, spread_ref, sems):
    n = a_ref.shape[0]
    nb = n // LANE
    trd = r_ref.shape[2]
    fetch = pltpu.make_async_copy(r_hbm, r_ref, sems.at[0])
    fetch.start()
    a_ref[:NB, :NB] = tiles_ref[:, 0].reshape(NB, NB)
    a_ref[NB:, :NB] = tiles_ref[:, 1].reshape(NB, NB)
    a_ref[NB:, NB:] = tiles_ref[:, 2].reshape(NB, NB)

    def blk(i):
        return slice(i * LANE, (i + 1) * LANE)

    inverses = []
    for b in range(nb):
        rows = [a_ref[b * LANE + SUB * g : b * LANE + SUB * (g + 1), blk(b)] for g in range(LANE // SUB)]
        upper, inverse = factor_block(rows, spread_ref)
        inverses.append(inverse)
        l_ref[blk(b), blk(b)] = upper
        for i in range(b + 1, nb):
            panel = dot_nt(a_ref[blk(i), blk(b)], inverse)
            l_ref[blk(i), blk(b)] = panel
            for j in range(b + 1, i + 1):
                a_ref[blk(i), blk(j)] = a_ref[blk(i), blk(j)] - dot_nt(panel, l_ref[blk(j), blk(b)])
        half, odd = divmod(b, 2)
        w_ref[2 * half, blk(odd), blk(odd)] = inverse
        if odd:
            w_ref[2 * half, blk(0), blk(1)] = jnp.zeros((LANE, LANE), jnp.float32)
            w_ref[2 * half, blk(1), blk(0)] = -dot_nn(inverse, dot_nn(l_ref[blk(b), blk(b - 1)], inverses[b - 1]))
        if b == 1:
            w_ref[1] = l_ref[NB:, :NB]
            fetch.wait()
            p0, p1 = (jnp.concatenate([r_ref[:, k, a].reshape(NB, NB) for a in range(trd)], 0) for k in range(2))
            s0 = dot6(split(p0), split(w_ref[0]))
            rest = p1 - dot6(split(s0), split(w_ref[1]))
            s_ref[:, :NB] = s0
    stores = [
        pltpu.make_async_copy(l_ref, l_hbm, sems.at[1]),
        pltpu.make_async_copy(w_ref, w_hbm, sems.at[2]),
        pltpu.make_async_copy(s_ref, s_hbm, sems.at[3]),
    ]
    for store in stores[:2]:
        store.start()
    s_ref[:, NB:] = dot6(split(rest), split(w_ref[2]))
    stores[2].start()
    for store in stores:
        store.wait()


def factor(tiles, r):
    n = 2 * NB
    trd = r.shape[1]
    hbm = pl.BlockSpec(memory_space=pltpu.HBM)
    r = r.reshape(Z, CORE, trd, PART, NB)
    shapes = [(n, n), (3, NB, NB), (trd * NB, n)]
    return pl.pallas_call(
        factor_kernel,
        out_shape=[jax.ShapeDtypeStruct(shape, jnp.float32) for shape in shapes],
        in_specs=[pl.BlockSpec(memory_space=pltpu.VMEM), hbm],
        out_specs=[hbm] * 3,
        scratch_shapes=[
            pltpu.VMEM((n, n), jnp.float32),
            pltpu.VMEM(shapes[0], jnp.float32),
            pltpu.VMEM(shapes[1], jnp.float32),
            pltpu.VMEM(r.shape, jnp.float32),
            pltpu.VMEM(shapes[2], jnp.float32),
            pltpu.VMEM((2 * SUB * (SUB + 2), LANE), jnp.float32),
            pltpu.SemaphoreType.DMA((4,)),
        ],
        compiler_params=pltpu.CompilerParams(vmem_limit_bytes=20 * 2**20),
        name="factor",
    )(tiles, r)


def update_kernel(
    place_ref, cov_hbm, g_hbm, w_hbm, l_hbm, left_hbm, out_ref, cov_ref, g_ref, w_ref, l_ref, left_ref, s_ref, sems
):
    trd, nb, tcd, _ = cov_ref.shape
    fetches = [pltpu.make_async_copy(w_hbm, w_ref, sems.at[0])]
    fetches += [pltpu.make_async_copy(g_hbm.at[:, :, a], g_ref.at[a], sems.at[1 + a]) for a in range(2)]
    fetches += [pltpu.make_async_copy(left_hbm, left_ref, sems.at[3]), pltpu.make_async_copy(cov_hbm, cov_ref, sems.at[4])]
    for fetch in fetches:
        fetch.start()
    fetches[0].wait()
    weights = [split(w_ref[i]) for i in range(3)]
    for a in range(2):
        fetches[1 + a].wait()
        p0, p1 = (
            jnp.concatenate([g_ref[a, 2 * h + k].reshape(NB, NB) for h in range(2)], 0) for k in range(2)
        )
        for k, parts in enumerate(solve(p0, p1, *weights)):
            for j, part in enumerate(parts):
                for h in range(2):
                    s_ref[j, 2 * a + h, :, k * NB : (k + 1) * NB] = part[h * NB : (h + 1) * NB]
    fetches[3].wait()
    left = split(left_ref[...])
    fetches[4].wait()
    for b in range(tcd):
        u = dot6(left, [s_ref[j, b] for j in range(3)])
        for a in range(trd):
            out_ref[a, :, b, :] = cov_ref[a, :, b, :] - u[a * nb : (a + 1) * nb]
    row, col = place_ref[0], place_ref[1]
    for k in range(2):

        @pl.when(col == k)
        def _():
            for a in range(trd):
                out_ref[a, :, 0, :] = left_ref[a * nb : (a + 1) * nb, k * NB : (k + 1) * NB]

    @pl.when(row < 2)
    def _():
        out_ref[0] = jnp.zeros_like(out_ref[0])

    for i in range(2):
        for j in range(i + 1):

            @pl.when(jnp.logical_and(row == i, col == j))
            def _():
                fetch = pltpu.make_async_copy(
                    l_hbm.at[i * NB : (i + 1) * NB, j * NB : (j + 1) * NB], l_ref, sems.at[5]
                )
                fetch.start()
                fetch.wait()
                for u in range(2):
                    for v in range(2):
                        if i == j and u < v:
                            continue
                        block = l_ref[u * LANE : (u + 1) * LANE, v * LANE : (v + 1) * LANE]
                        out_ref[0, u * LANE : (u + 1) * LANE, 0, v * LANE : (v + 1) * LANE] = (
                            block.T if i == j and u == v else block
                        )


def update(place, cov, g, w, lower, left):
    trd, nb, tcd, _ = cov.shape
    hbm = pl.BlockSpec(memory_space=pltpu.HBM)
    return pl.pallas_call(
        update_kernel,
        out_shape=jax.ShapeDtypeStruct(cov.shape, jnp.float32),
        in_specs=[pl.BlockSpec(memory_space=pltpu.SMEM)] + [hbm] * 5,
        out_specs=pl.BlockSpec(memory_space=pltpu.VMEM),
        scratch_shapes=[
            pltpu.VMEM(cov.shape, jnp.float32),
            pltpu.VMEM((2, X, Y, PART, NB), jnp.float32),
            pltpu.VMEM(w.shape, jnp.float32),
            pltpu.VMEM((NB, NB), jnp.float32),
            pltpu.VMEM(left.shape, jnp.float32),
            pltpu.VMEM((3, tcd, nb, 2 * nb), jnp.bfloat16),
            pltpu.SemaphoreType.DMA((6,)),
        ],
        compiler_params=pltpu.CompilerParams(vmem_limit_bytes=24 * 2**20),
        name="update",
    )(place, cov, g, w, lower, left)


def shared(block, groups):
    many = jnp.broadcast_to(block[None], (len(groups[0]),) + block.shape)
    return lax.all_to_all(many, "row", 0, 0, axis_index_groups=groups)


def on_device(cov):
    row, col = lax.axis_index("row"), lax.axis_index("col")
    x, y, z = row // Y, row % Y, col // CORE
    along_x = [[i * Y + j for i in range(X)] for j in range(Y)]
    along_y = [[i * Y + j for j in range(Y)] for i in range(X)]
    chips = [[c * CORE + k for k in range(CORE)] for c in range(Z)]
    panel = cov[:, :, 0, :]

    tile = panel[0].reshape(X, NB // X, NB)
    head = jnp.where(x == 0, tile[0], 0.0)
    for s in range(1, X):
        pairs = [(device(0, j, 0, k), device(s, j, 0, k)) for j, k in ROOTS]
        head = head + lax.ppermute(tile[s], BOTH, pairs)

    parts = panel.reshape(2, Z, PART, NB)
    mine = jnp.where(z == 0, parts[:, 0], 0.0)
    for s in range(1, Z):
        pairs = [(p * N_COL + k, p * N_COL + s * CORE + k) for p in range(N_ROW) for k in range(CORE)]
        mine = mine + lax.ppermute(parts[:, s], BOTH, pairs)
    r = lax.all_gather(mine, "col")

    pairs = [
        (p * N_COL + c * CORE + k, device(2 * (p // N_COL) + k, c, (p % N_COL) // CORE, p % CORE))
        for p in range(N_ROW)
        for c in range(Z)
        for k in range(CORE)
    ]
    moved = lax.ppermute(mine, BOTH, pairs)

    first = jnp.where(y == 0, head, 0.0)
    second = jnp.where(y == 1, head, 0.0)
    for s in range(1, Y):
        pairs = [(device(i, j, 0, k), device(i, (j + s) % Y, 0, k)) for i in range(X) for j, k in ROOTS]
        came = lax.ppermute(head, BOTH, pairs)
        first = jnp.where(y == s, came, first)
        second = jnp.where(y == (s + 1) % Y, came, second)
    here = jnp.stack([first, second])
    moved, here = lax.optimization_barrier((moved, here))
    head = jnp.where(z == 0, here, 0.0)
    for s in range(1, Z):
        pairs = [(device(i, j, 0, k), device(i, j, s, k)) for i in range(X) for j in range(Y) for k in range(CORE)]
        head = head + lax.ppermute(here, BOTH, pairs)

    got = shared(moved, along_y)
    g = lax.all_gather(got, "row", axis_index_groups=along_x)

    head = lax.all_gather(head, "col", axis_index_groups=chips)
    tiles = shared(jnp.stack([head[0, 0], head[0, 1], head[1, 1]]), along_x)
    lower, w, left = factor(tiles, r)
    return update(jnp.stack([row, col]).astype(jnp.int32), cov, g, w, lower, left)


def solution(mesh):
    placed = (P(None, "row", None, "col"),)
    return jax.shard_map(
        on_device,
        mesh=mesh,
        in_specs=placed,
        out_specs=P(None, "row", None, "col"),
        check_vma=False,
    )
```

```python
import jax
import jax.numpy as jnp
from jax import lax
from jax.experimental import pallas as pl
from jax.experimental.pallas import tpu as pltpu
from jax.sharding import PartitionSpec as P

LANE = 128
SUB = 8
X, Y, Z, CORE = 4, 8, 8, 2
N_ROW, N_COL = X * Y, Z * CORE
NB = 256
PART = NB // Z
BOTH = ("row", "col")
VMEM_LIMIT = 24 * 2**20
ROOTS = ((0, 0), (1, 0), (1, 1))


def device(x, y, z, core):
    return (x * Y + y) * N_COL + z * CORE + core


def dot_nt(a, b):
    return lax.dot_general(
        a, b, (((1,), (1,)), ((), ())), precision=lax.Precision.HIGHEST, preferred_element_type=jnp.float32
    )


def dot_nn(a, b):
    return lax.dot_general(
        a, b, (((1,), (0,)), ((), ())), precision=lax.Precision.HIGHEST, preferred_element_type=jnp.float32
    )


def column(rows, k):
    return jnp.broadcast_to(rows[:, k : k + 1], (SUB, LANE))


def total(terms):
    terms = list(terms)
    while len(terms) > 1:
        terms = [sum(terms[i : i + 2]) for i in range(0, len(terms), 2)]
    return terms[0]


def factor_block(rows, s_ref):
    count = len(rows)
    rows = list(rows)
    sub = lax.broadcasted_iota(jnp.int32, (SUB, LANE), 0)
    lane = lax.broadcasted_iota(jnp.int32, (SUB, LANE), 1)
    aug = [jnp.where(lane == sub + SUB * g, 1.0, 0.0).astype(jnp.float32) for g in range(count)]
    span = SUB * (SUB + 2)
    for p in range(count):
        base = (p % 2) * span
        for k in range(SUB):
            s_ref[base + SUB * k : base + SUB * (k + 1), :] = column(rows[p], SUB * p + k)
        s_ref[base + SUB * SUB : base + SUB * (SUB + 1), :] = rows[p]
        s_ref[base + SUB * (SUB + 1) : base + span, :] = aug[p]

        def spread(i, base=base):
            return jnp.broadcast_to(s_ref[base + i : base + i + 1, :], (SUB, LANE))

        a = {(m, k): spread(SUB * k + m) for k in range(SUB) for m in range(k, SUB)}
        low, scale = {}, []
        for k in range(0, SUB, 2):
            first, cross, second = a[k, k], a[k + 1, k], a[k + 1, k + 1]
            r1 = lax.rsqrt(first)
            r2 = lax.rsqrt(first * second - cross * cross) * (first * r1)
            scale += [r1, r2]
            low[k + 1, k] = cross * r1
            for m in range(k + 2, SUB):
                low[m, k] = a[m, k] * r1
                low[m, k + 1] = (a[m, k + 1] - low[m, k] * low[k + 1, k]) * r2
            for m in range(k + 2, SUB):
                for n in range(k + 2, m + 1):
                    a[m, n] = a[m, n] - (low[m, k] * low[n, k] + low[m, k + 1] * low[n, k + 1])
        xs, ys = [], []
        for k in range(SUB):
            x, y = spread(SUB * SUB + k), spread(SUB * (SUB + 1) + k)
            for j in range(k):
                x = x - low[k, j] * xs[j]
                y = y - low[k, j] * ys[j]
            xs.append(x * scale[k])
            ys.append(y * scale[k])
        for g in range(p + 1, count):
            left = []
            for k in range(SUB):
                t = column(rows[g], SUB * p + k)
                for j in range(k):
                    t = t - left[j] * low[k, j]
                left.append(t * scale[k])
            rows[g] = rows[g] - total(c * x for c, x in zip(left, xs))
            aug[g] = aug[g] - total(c * y for c, y in zip(left, ys))
        x, y = xs[0], ys[0]
        for k in range(1, SUB):
            x = jnp.where(sub == k, xs[k], x)
            y = jnp.where(sub == k, ys[k], y)
        rows[p] = jnp.where(lane >= sub + SUB * p, x, 0.0)
        aug[p] = y
    return jnp.concatenate(rows, 0), jnp.concatenate(aug, 0)


def split(x):
    hi = x.astype(jnp.bfloat16)
    rest = x - hi.astype(jnp.float32)
    mid = rest.astype(jnp.bfloat16)
    return hi, mid, (rest - mid.astype(jnp.float32)).astype(jnp.bfloat16)


def dot6(a, b):
    out = None
    for i in range(3):
        for j in range(3 - i):
            t = lax.dot_general(a[i], b[j], (((1,), (1,)), ((), ())), preferred_element_type=jnp.float32)
            out = t if out is None else out + t
    return out


def solve(p0, p1, w0, l10, w1):
    a0 = split(dot6(split(p0), w0))
    return a0, split(dot6(split(p1 - dot6(a0, l10)), w1))


def factor_kernel(tiles_ref, r_hbm, l_ref, w_ref, s_ref, a_ref, r_ref, spread_ref, sem):
    n = a_ref.shape[0]
    nb = n // LANE
    trd = r_ref.shape[2]
    fetch = pltpu.make_async_copy(r_hbm, r_ref, sem)
    fetch.start()
    a_ref[:NB, :NB] = tiles_ref[:, 0].reshape(NB, NB)
    a_ref[NB:, :NB] = tiles_ref[:, 1].reshape(NB, NB)
    a_ref[NB:, NB:] = tiles_ref[:, 2].reshape(NB, NB)

    def blk(i):
        return slice(i * LANE, (i + 1) * LANE)

    inverses = []
    for b in range(nb):
        rows = [a_ref[b * LANE + SUB * g : b * LANE + SUB * (g + 1), blk(b)] for g in range(LANE // SUB)]
        upper, inverse = factor_block(rows, spread_ref)
        inverses.append(inverse)
        l_ref[blk(b), blk(b)] = upper
        for i in range(b + 1, nb):
            panel = dot_nt(a_ref[blk(i), blk(b)], inverse)
            l_ref[blk(i), blk(b)] = panel
            for j in range(b + 1, i + 1):
                a_ref[blk(i), blk(j)] = a_ref[blk(i), blk(j)] - dot_nt(panel, l_ref[blk(j), blk(b)])
        half, odd = divmod(b, 2)
        w_ref[2 * half, blk(odd), blk(odd)] = inverse
        if odd:
            w_ref[2 * half, blk(0), blk(1)] = jnp.zeros((LANE, LANE), jnp.float32)
            w_ref[2 * half, blk(1), blk(0)] = -dot_nn(inverse, dot_nn(l_ref[blk(b), blk(b - 1)], inverses[b - 1]))
        if b == 1:
            w_ref[1] = l_ref[NB:, :NB]
            fetch.wait()
            p0, p1 = (jnp.concatenate([r_ref[:, k, a].reshape(NB, NB) for a in range(trd)], 0) for k in range(2))
            s0 = dot6(split(p0), split(w_ref[0]))
            rest = p1 - dot6(split(s0), split(w_ref[1]))
            s_ref[:, :NB] = s0
    s_ref[:, NB:] = dot6(split(rest), split(w_ref[2]))


def factor(tiles, r):
    n = 2 * NB
    trd = r.shape[1]
    vmem = pl.BlockSpec(memory_space=pltpu.VMEM)
    r = pltpu.with_memory_space_constraint(r.reshape(Z, CORE, trd, PART, NB), pltpu.HBM)
    shapes = [(n, n), (3, NB, NB), (trd * NB, n)]
    return pl.pallas_call(
        factor_kernel,
        out_shape=[jax.ShapeDtypeStruct(shape, jnp.float32) for shape in shapes],
        in_specs=[vmem, pl.BlockSpec(memory_space=pltpu.HBM)],
        out_specs=[vmem] * 3,
        scratch_shapes=[
            pltpu.VMEM((n, n), jnp.float32),
            pltpu.VMEM(r.shape, jnp.float32),
            pltpu.VMEM((2 * SUB * (SUB + 2), LANE), jnp.float32),
            pltpu.SemaphoreType.DMA,
        ],
        compiler_params=pltpu.CompilerParams(vmem_limit_bytes=VMEM_LIMIT),
        name="factor",
    )(tiles, r)


def update_kernel(
    place_ref, cov_ref, g_hbm, w_hbm, l_hbm, left_hbm, out_ref, g_ref, w_ref, l_ref, left_ref, s_ref, sems
):
    trd, nb, tcd, _ = cov_ref.shape
    fetches = [pltpu.make_async_copy(w_hbm, w_ref, sems.at[0])]
    fetches += [pltpu.make_async_copy(g_hbm.at[:, :, a], g_ref.at[a], sems.at[1 + a]) for a in range(2)]
    fetches.append(pltpu.make_async_copy(left_hbm, left_ref, sems.at[3]))
    for fetch in fetches:
        fetch.start()
    fetches[0].wait()
    weights = [split(w_ref[i]) for i in range(3)]
    for a in range(2):
        fetches[1 + a].wait()
        p0, p1 = (
            jnp.concatenate([g_ref[a, 2 * h + k].reshape(NB, NB) for h in range(2)], 0) for k in range(2)
        )
        for k, parts in enumerate(solve(p0, p1, *weights)):
            for j, part in enumerate(parts):
                for h in range(2):
                    s_ref[j, 2 * a + h, :, k * NB : (k + 1) * NB] = part[h * NB : (h + 1) * NB]
    fetches[3].wait()
    left = split(left_ref[...])
    for b in range(tcd):
        u = dot6(left, [s_ref[j, b] for j in range(3)])
        for a in range(trd):
            out_ref[a, :, b, :] = cov_ref[a, :, b, :] - u[a * nb : (a + 1) * nb]
    row, col = place_ref[0], place_ref[1]
    for k in range(2):

        @pl.when(col == k)
        def _():
            for a in range(trd):
                out_ref[a, :, 0, :] = left_ref[a * nb : (a + 1) * nb, k * NB : (k + 1) * NB]

    @pl.when(row < 2)
    def _():
        out_ref[0] = jnp.zeros_like(out_ref[0])

    for i in range(2):
        for j in range(i + 1):

            @pl.when(jnp.logical_and(row == i, col == j))
            def _():
                fetch = pltpu.make_async_copy(
                    l_hbm.at[i * NB : (i + 1) * NB, j * NB : (j + 1) * NB], l_ref, sems.at[4]
                )
                fetch.start()
                fetch.wait()
                for u in range(2):
                    for v in range(2):
                        if i == j and u < v:
                            continue
                        block = l_ref[u * LANE : (u + 1) * LANE, v * LANE : (v + 1) * LANE]
                        out_ref[0, u * LANE : (u + 1) * LANE, 0, v * LANE : (v + 1) * LANE] = (
                            block.T if i == j and u == v else block
                        )


def update(place, cov, *rest):
    trd, nb, tcd, _ = cov.shape
    vmem, hbm = (pl.BlockSpec(memory_space=space) for space in (pltpu.VMEM, pltpu.HBM))
    rest = [pltpu.with_memory_space_constraint(array, pltpu.HBM) for array in rest]
    g, w, _, left = rest
    return pl.pallas_call(
        update_kernel,
        out_shape=jax.ShapeDtypeStruct(cov.shape, jnp.float32),
        in_specs=[pl.BlockSpec(memory_space=pltpu.SMEM), vmem] + [hbm] * len(rest),
        out_specs=vmem,
        scratch_shapes=[
            pltpu.VMEM((2, X, Y, PART, NB), jnp.float32),
            pltpu.VMEM(w.shape, jnp.float32),
            pltpu.VMEM((NB, NB), jnp.float32),
            pltpu.VMEM(left.shape, jnp.float32),
            pltpu.VMEM((3, tcd, nb, 2 * nb), jnp.bfloat16),
            pltpu.SemaphoreType.DMA((5,)),
        ],
        compiler_params=pltpu.CompilerParams(vmem_limit_bytes=VMEM_LIMIT),
        name="update",
    )(place, cov, *rest)


def shared(block, axis, groups):
    many = jnp.broadcast_to(block[None], (len(groups[0]),) + block.shape)
    return lax.all_to_all(many, axis, 0, 0, axis_index_groups=groups)


def on_device(cov):
    row, col = lax.axis_index("row"), lax.axis_index("col")
    x, y, z = row // Y, row % Y, col // CORE
    along_x = [[i * Y + j for i in range(X)] for j in range(Y)]
    along_y = [[i * Y + j for j in range(Y)] for i in range(X)]
    along_z = [[c * CORE + k for c in range(Z)] for k in range(CORE)]
    chips = [[c * CORE + k for k in range(CORE)] for c in range(Z)]
    panel = cov[:, :, 0, :].reshape(2, Z, PART, NB)

    mine = jnp.where(z == 0, panel[:, 0], 0.0)
    for s in range(1, Z):
        pairs = [(p * N_COL + k, p * N_COL + s * CORE + k) for p in range(N_ROW) for k in range(CORE)]
        mine = mine + lax.ppermute(panel[:, s], BOTH, pairs)
    r = lax.all_gather(mine, "col")

    pairs = [
        (p * N_COL + c * CORE + k, device(2 * (p // N_COL) + k, c, (p % N_COL) // CORE, p % CORE))
        for p in range(N_ROW)
        for c in range(Z)
        for k in range(CORE)
    ]
    moved = lax.ppermute(mine, BOTH, pairs)
    got = shared(moved, "row", along_y)

    head = jnp.where(x == 0, mine[0], 0.0)
    for s in range(1, X):
        pairs = [(device(0, j, c, k), device(s, j, c, k)) for c in range(Z) for j, k in ROOTS]
        head = head + lax.ppermute(mine[0], BOTH, pairs)
    first = jnp.where(y == 0, head, 0.0)
    second = jnp.where(y == 1, head, 0.0)
    for s in range(1, Y):
        pairs = [
            (device(i, j, c, k), device(i, (j + s) % Y, c, k)) for i in range(X) for c in range(Z) for j, k in ROOTS
        ]
        came = lax.ppermute(head, BOTH, pairs)
        first = jnp.where(y == s, came, first)
        second = jnp.where(y == (s + 1) % Y, came, second)

    head = lax.all_gather(jnp.stack([first, second]), "col", axis_index_groups=chips)
    tiles = shared(jnp.stack([head[0, 0], head[0, 1], head[1, 1]]), "col", along_z)
    got, tiles = lax.optimization_barrier((got, tiles))
    g = lax.all_gather(got, "row", axis_index_groups=along_x)
    lower, w, left = factor(tiles, r)
    return update(jnp.stack([row, col]).astype(jnp.int32), cov, g, w, lower, left)


def solution(mesh):
    placed = (P(None, "row", None, "col"),)
    return jax.shard_map(
        on_device,
        mesh=mesh,
        in_specs=placed,
        out_specs=P(None, "row", None, "col"),
        check_vma=False,
    )
```

```python
import jax
import jax.numpy as jnp
from jax import lax
from jax.experimental import pallas as pl
from jax.experimental.pallas import tpu as pltpu
from jax.sharding import PartitionSpec as P

LANE = 128
SUB = 8
X, Y, Z, CORE = 4, 8, 8, 2
N_ROW, N_COL = X * Y, Z * CORE
NB = 256
PART = NB // Z
BOTH = ("row", "col")
VMEM_LIMIT = 24 * 2**20
ROOTS = ((0, 0), (1, 0), (1, 1))


def device(x, y, z, core):
    return (x * Y + y) * N_COL + z * CORE + core


def dot_nt(a, b):
    return lax.dot_general(
        a, b, (((1,), (1,)), ((), ())), precision=lax.Precision.HIGHEST, preferred_element_type=jnp.float32
    )


def dot_nn(a, b):
    return lax.dot_general(
        a, b, (((1,), (0,)), ((), ())), precision=lax.Precision.HIGHEST, preferred_element_type=jnp.float32
    )


def column(rows, k):
    return jnp.broadcast_to(rows[:, k : k + 1], (SUB, LANE))


def total(terms):
    terms = list(terms)
    while len(terms) > 1:
        terms = [sum(terms[i : i + 2]) for i in range(0, len(terms), 2)]
    return terms[0]


def factor_block(rows, s_ref):
    count = len(rows)
    rows = list(rows)
    sub = lax.broadcasted_iota(jnp.int32, (SUB, LANE), 0)
    lane = lax.broadcasted_iota(jnp.int32, (SUB, LANE), 1)
    aug = [jnp.where(lane == sub + SUB * g, 1.0, 0.0).astype(jnp.float32) for g in range(count)]
    span = SUB * (SUB + 2)
    for p in range(count):
        base = (p % 2) * span
        for k in range(SUB):
            s_ref[base + SUB * k : base + SUB * (k + 1), :] = column(rows[p], SUB * p + k)
        s_ref[base + SUB * SUB : base + SUB * (SUB + 1), :] = rows[p]
        s_ref[base + SUB * (SUB + 1) : base + span, :] = aug[p]

        def spread(i, base=base):
            return jnp.broadcast_to(s_ref[base + i : base + i + 1, :], (SUB, LANE))

        a = {(m, k): spread(SUB * k + m) for k in range(SUB) for m in range(k, SUB)}
        low, scale = {}, []
        for k in range(0, SUB, 2):
            first, cross, second = a[k, k], a[k + 1, k], a[k + 1, k + 1]
            r1 = lax.rsqrt(first)
            r2 = lax.rsqrt(first * second - cross * cross) * (first * r1)
            scale += [r1, r2]
            low[k + 1, k] = cross * r1
            for m in range(k + 2, SUB):
                low[m, k] = a[m, k] * r1
                low[m, k + 1] = (a[m, k + 1] - low[m, k] * low[k + 1, k]) * r2
            for m in range(k + 2, SUB):
                for n in range(k + 2, m + 1):
                    a[m, n] = a[m, n] - (low[m, k] * low[n, k] + low[m, k + 1] * low[n, k + 1])
        xs, ys = [], []
        for k in range(SUB):
            x, y = spread(SUB * SUB + k), spread(SUB * (SUB + 1) + k)
            for j in range(k):
                x = x - low[k, j] * xs[j]
                y = y - low[k, j] * ys[j]
            xs.append(x * scale[k])
            ys.append(y * scale[k])
        for g in range(p + 1, count):
            left = []
            for k in range(SUB):
                t = column(rows[g], SUB * p + k)
                for j in range(k):
                    t = t - left[j] * low[k, j]
                left.append(t * scale[k])
            rows[g] = rows[g] - total(c * x for c, x in zip(left, xs))
            aug[g] = aug[g] - total(c * y for c, y in zip(left, ys))
        x, y = xs[0], ys[0]
        for k in range(1, SUB):
            x = jnp.where(sub == k, xs[k], x)
            y = jnp.where(sub == k, ys[k], y)
        rows[p] = jnp.where(lane >= sub + SUB * p, x, 0.0)
        aug[p] = y
    return jnp.concatenate(rows, 0), jnp.concatenate(aug, 0)


def split(x):
    hi = x.astype(jnp.bfloat16)
    rest = x - hi.astype(jnp.float32)
    mid = rest.astype(jnp.bfloat16)
    return hi, mid, (rest - mid.astype(jnp.float32)).astype(jnp.bfloat16)


def dot6(a, b):
    out = None
    for i in range(3):
        for j in range(3 - i):
            t = lax.dot_general(a[i], b[j], (((1,), (1,)), ((), ())), preferred_element_type=jnp.float32)
            out = t if out is None else out + t
    return out


def solve(p0, p1, w0, l10, w1):
    a0 = split(dot6(split(p0), w0))
    return a0, split(dot6(split(p1 - dot6(a0, l10)), w1))


def factor_kernel(tiles_ref, r_hbm, l_ref, w_ref, s_ref, a_ref, r_ref, spread_ref, sem):
    n = a_ref.shape[0]
    nb = n // LANE
    trd = r_ref.shape[2]
    fetch = pltpu.make_async_copy(r_hbm, r_ref, sem)
    fetch.start()
    a_ref[:NB, :NB] = tiles_ref[:, 0].reshape(NB, NB)
    a_ref[NB:, :NB] = tiles_ref[:, 1].reshape(NB, NB)
    a_ref[NB:, NB:] = tiles_ref[:, 2].reshape(NB, NB)

    def blk(i):
        return slice(i * LANE, (i + 1) * LANE)

    inverses = []
    for b in range(nb):
        rows = [a_ref[b * LANE + SUB * g : b * LANE + SUB * (g + 1), blk(b)] for g in range(LANE // SUB)]
        upper, inverse = factor_block(rows, spread_ref)
        inverses.append(inverse)
        l_ref[blk(b), blk(b)] = upper
        for i in range(b + 1, nb):
            panel = dot_nt(a_ref[blk(i), blk(b)], inverse)
            l_ref[blk(i), blk(b)] = panel
            for j in range(b + 1, i + 1):
                a_ref[blk(i), blk(j)] = a_ref[blk(i), blk(j)] - dot_nt(panel, l_ref[blk(j), blk(b)])
        half, odd = divmod(b, 2)
        w_ref[2 * half, blk(odd), blk(odd)] = inverse
        if odd:
            w_ref[2 * half, blk(0), blk(1)] = jnp.zeros((LANE, LANE), jnp.float32)
            w_ref[2 * half, blk(1), blk(0)] = -dot_nn(inverse, dot_nn(l_ref[blk(b), blk(b - 1)], inverses[b - 1]))
        if b == 1:
            w_ref[1] = l_ref[NB:, :NB]
            fetch.wait()
            p0, p1 = (jnp.concatenate([r_ref[:, k, a].reshape(NB, NB) for a in range(trd)], 0) for k in range(2))
            s0 = dot6(split(p0), split(w_ref[0]))
            rest = p1 - dot6(split(s0), split(w_ref[1]))
            s_ref[:, :NB] = s0
    s_ref[:, NB:] = dot6(split(rest), split(w_ref[2]))


def factor(tiles, r):
    n = 2 * NB
    trd = r.shape[1]
    vmem = pl.BlockSpec(memory_space=pltpu.VMEM)
    r = pltpu.with_memory_space_constraint(r.reshape(Z, CORE, trd, PART, NB), pltpu.HBM)
    shapes = [(n, n), (3, NB, NB), (trd * NB, n)]
    return pl.pallas_call(
        factor_kernel,
        out_shape=[jax.ShapeDtypeStruct(shape, jnp.float32) for shape in shapes],
        in_specs=[vmem, pl.BlockSpec(memory_space=pltpu.HBM)],
        out_specs=[vmem] * 3,
        scratch_shapes=[
            pltpu.VMEM((n, n), jnp.float32),
            pltpu.VMEM(r.shape, jnp.float32),
            pltpu.VMEM((2 * SUB * (SUB + 2), LANE), jnp.float32),
            pltpu.SemaphoreType.DMA,
        ],
        compiler_params=pltpu.CompilerParams(vmem_limit_bytes=VMEM_LIMIT),
        name="factor",
    )(tiles, r)


def update_kernel(
    place_ref, cov_ref, g_hbm, w_hbm, l_hbm, left_hbm, out_ref, g_ref, w_ref, l_ref, left_ref, s_ref, sems
):
    trd, nb, tcd, _ = cov_ref.shape
    fetches = [pltpu.make_async_copy(w_hbm, w_ref, sems.at[0])]
    fetches += [pltpu.make_async_copy(g_hbm.at[:, :, a], g_ref.at[a], sems.at[1 + a]) for a in range(2)]
    fetches.append(pltpu.make_async_copy(left_hbm, left_ref, sems.at[3]))
    for fetch in fetches:
        fetch.start()
    fetches[0].wait()
    weights = [split(w_ref[i]) for i in range(3)]
    for a in range(2):
        fetches[1 + a].wait()
        p0, p1 = (
            jnp.concatenate([g_ref[a, 2 * h + k].reshape(NB, NB) for h in range(2)], 0) for k in range(2)
        )
        for k, parts in enumerate(solve(p0, p1, *weights)):
            for j, part in enumerate(parts):
                for h in range(2):
                    s_ref[j, 2 * a + h, :, k * NB : (k + 1) * NB] = part[h * NB : (h + 1) * NB]
    fetches[3].wait()
    left = split(left_ref[...])
    for b in range(tcd):
        u = dot6(left, [s_ref[j, b] for j in range(3)])
        for a in range(trd):
            out_ref[a, :, b, :] = cov_ref[a, :, b, :] - u[a * nb : (a + 1) * nb]
    row, col = place_ref[0], place_ref[1]
    for k in range(2):

        @pl.when(col == k)
        def _():
            for a in range(trd):
                out_ref[a, :, 0, :] = left_ref[a * nb : (a + 1) * nb, k * NB : (k + 1) * NB]

    @pl.when(row < 2)
    def _():
        out_ref[0] = jnp.zeros_like(out_ref[0])

    for i in range(2):
        for j in range(i + 1):

            @pl.when(jnp.logical_and(row == i, col == j))
            def _():
                fetch = pltpu.make_async_copy(
                    l_hbm.at[i * NB : (i + 1) * NB, j * NB : (j + 1) * NB], l_ref, sems.at[4]
                )
                fetch.start()
                fetch.wait()
                for u in range(2):
                    for v in range(2):
                        if i == j and u < v:
                            continue
                        block = l_ref[u * LANE : (u + 1) * LANE, v * LANE : (v + 1) * LANE]
                        out_ref[0, u * LANE : (u + 1) * LANE, 0, v * LANE : (v + 1) * LANE] = (
                            block.T if i == j and u == v else block
                        )


def update(place, cov, *rest):
    trd, nb, tcd, _ = cov.shape
    vmem, hbm = (pl.BlockSpec(memory_space=space) for space in (pltpu.VMEM, pltpu.HBM))
    rest = [pltpu.with_memory_space_constraint(array, pltpu.HBM) for array in rest]
    g, w, _, left = rest
    return pl.pallas_call(
        update_kernel,
        out_shape=jax.ShapeDtypeStruct(cov.shape, jnp.float32),
        in_specs=[pl.BlockSpec(memory_space=pltpu.SMEM), vmem] + [hbm] * len(rest),
        out_specs=vmem,
        scratch_shapes=[
            pltpu.VMEM((2, X, Y, PART, NB), jnp.float32),
            pltpu.VMEM(w.shape, jnp.float32),
            pltpu.VMEM((NB, NB), jnp.float32),
            pltpu.VMEM(left.shape, jnp.float32),
            pltpu.VMEM((3, tcd, nb, 2 * nb), jnp.bfloat16),
            pltpu.SemaphoreType.DMA((5,)),
        ],
        compiler_params=pltpu.CompilerParams(vmem_limit_bytes=VMEM_LIMIT),
        name="update",
    )(place, cov, *rest)


def shared(block, axis, groups):
    many = jnp.broadcast_to(block[None], (len(groups[0]),) + block.shape)
    return lax.all_to_all(many, axis, 0, 0, axis_index_groups=groups)


def on_device(cov):
    row, col = lax.axis_index("row"), lax.axis_index("col")
    x, z = row // Y, col // CORE
    along_x = [[i * Y + j for i in range(X)] for j in range(Y)]
    along_y = [[i * Y + j for j in range(Y)] for i in range(X)]
    along_z = [[c * CORE + k for c in range(Z)] for k in range(CORE)]
    chips = [[c * CORE + k for k in range(CORE)] for c in range(Z)]
    panel = cov[:, :, 0, :].reshape(2, Z, PART, NB)

    mine = jnp.where(z == 0, panel[:, 0], 0.0)
    for s in range(1, Z):
        pairs = [(p * N_COL + k, p * N_COL + s * CORE + k) for p in range(N_ROW) for k in range(CORE)]
        mine = mine + lax.ppermute(panel[:, s], BOTH, pairs)
    r = lax.all_gather(mine, "col")

    pairs = [
        (p * N_COL + c * CORE + k, device(2 * (p // N_COL) + k, c, (p % N_COL) // CORE, p % CORE))
        for p in range(N_ROW)
        for c in range(Z)
        for k in range(CORE)
    ]
    moved = lax.ppermute(mine, BOTH, pairs)

    head = jnp.where(x == 0, mine[0], 0.0)
    for s in range(1, X):
        pairs = [(device(0, j, c, k), device(s, j, c, k)) for c in range(Z) for j, k in ROOTS]
        head = head + lax.ppermute(mine[0], BOTH, pairs)
    got = shared(jnp.concatenate([moved, head[None]]), "row", along_y)
    g = lax.all_gather(got[:, :2], "row", axis_index_groups=along_x)

    head = lax.all_gather(got[:2, 2], "col", axis_index_groups=chips)
    tiles = shared(jnp.stack([head[0, 0], head[0, 1], head[1, 1]]), "col", along_z)
    lower, w, left = factor(tiles, r)
    return update(jnp.stack([row, col]).astype(jnp.int32), cov, g, w, lower, left)


def solution(mesh):
    placed = (P(None, "row", None, "col"),)
    return jax.shard_map(
        on_device,
        mesh=mesh,
        in_specs=placed,
        out_specs=P(None, "row", None, "col"),
        check_vma=False,
    )
```

```python
import jax
import jax.numpy as jnp
from jax import lax
from jax.experimental import pallas as pl
from jax.experimental.pallas import tpu as pltpu
from jax.sharding import PartitionSpec as P

LANE = 128
SUB = 8
X, Y, Z, CORE = 4, 8, 8, 2
N_ROW, N_COL = X * Y, Z * CORE
NB = 256
PART = NB // Z
BOTH = ("row", "col")
ROOTS = ((0, 0), (1, 0), (1, 1))


def device(x, y, z, core):
    return (x * Y + y) * N_COL + z * CORE + core


def dot_nt(a, b):
    return lax.dot_general(
        a, b, (((1,), (1,)), ((), ())), precision=lax.Precision.HIGHEST, preferred_element_type=jnp.float32
    )


def dot_nn(a, b):
    return lax.dot_general(
        a, b, (((1,), (0,)), ((), ())), precision=lax.Precision.HIGHEST, preferred_element_type=jnp.float32
    )


def column(rows, k):
    return jnp.broadcast_to(rows[:, k : k + 1], (SUB, LANE))


def total(terms):
    terms = list(terms)
    while len(terms) > 1:
        terms = [sum(terms[i : i + 2]) for i in range(0, len(terms), 2)]
    return terms[0]


def factor_block(rows, s_ref, between):
    count = len(rows)
    rows = list(rows)
    sub = lax.broadcasted_iota(jnp.int32, (SUB, LANE), 0)
    lane = lax.broadcasted_iota(jnp.int32, (SUB, LANE), 1)
    aug = [jnp.where(lane == sub + SUB * g, 1.0, 0.0).astype(jnp.float32) for g in range(count)]
    span = SUB * (SUB + 2)
    for p in range(count):
        base = (p % 2) * span
        for k in range(SUB):
            s_ref[base + SUB * k : base + SUB * (k + 1), :] = column(rows[p], SUB * p + k)
        s_ref[base + SUB * SUB : base + SUB * (SUB + 1), :] = rows[p]
        s_ref[base + SUB * (SUB + 1) : base + span, :] = aug[p]

        def spread(i, base=base):
            return jnp.broadcast_to(s_ref[base + i : base + i + 1, :], (SUB, LANE))

        a = {(m, k): spread(SUB * k + m) for k in range(SUB) for m in range(k, SUB)}
        low, scale = {}, []
        for k in range(0, SUB, 2):
            first, cross, second = a[k, k], a[k + 1, k], a[k + 1, k + 1]
            r1 = lax.rsqrt(first)
            r2 = lax.rsqrt(first * second - cross * cross) * (first * r1)
            scale += [r1, r2]
            low[k + 1, k] = cross * r1
            for m in range(k + 2, SUB):
                low[m, k] = a[m, k] * r1
                low[m, k + 1] = (a[m, k + 1] - low[m, k] * low[k + 1, k]) * r2
            for m in range(k + 2, SUB):
                for n in range(k + 2, m + 1):
                    a[m, n] = a[m, n] - (low[m, k] * low[n, k] + low[m, k + 1] * low[n, k + 1])
        xs, ys = [], []
        for k in range(SUB):
            x, y = spread(SUB * SUB + k), spread(SUB * (SUB + 1) + k)
            for j in range(k):
                x = x - low[k, j] * xs[j]
                y = y - low[k, j] * ys[j]
            xs.append(x * scale[k])
            ys.append(y * scale[k])
        for g in range(p + 1, count):
            left = []
            for k in range(SUB):
                t = column(rows[g], SUB * p + k)
                for j in range(k):
                    t = t - left[j] * low[k, j]
                left.append(t * scale[k])
            rows[g] = rows[g] - total(c * x for c, x in zip(left, xs))
            aug[g] = aug[g] - total(c * y for c, y in zip(left, ys))
        x, y = xs[0], ys[0]
        for k in range(1, SUB):
            x = jnp.where(sub == k, xs[k], x)
            y = jnp.where(sub == k, ys[k], y)
        rows[p] = jnp.where(lane >= sub + SUB * p, x, 0.0)
        aug[p] = y
        between()
    return jnp.concatenate(rows, 0), jnp.concatenate(aug, 0)


def split(x):
    hi = x.astype(jnp.bfloat16)
    rest = x - hi.astype(jnp.float32)
    mid = rest.astype(jnp.bfloat16)
    return hi, mid, (rest - mid.astype(jnp.float32)).astype(jnp.bfloat16)


def dot6(a, b):
    out = None
    for i in range(3):
        for j in range(3 - i):
            t = lax.dot_general(a[i], b[j], (((1,), (1,)), ((), ())), preferred_element_type=jnp.float32)
            out = t if out is None else out + t
    return out


def head_and_update_kernel(
    place_ref, cov_ref, mine_hbm, other_hbm, r_hbm, g_hbm, out_ref,
    tiles_ref, r_ref, g_ref, a_ref, l_ref, w_ref, s0_ref, t_ref, s1_ref, spread_ref, sems,
):
    trd, nb, tcd, _ = cov_ref.shape
    row, col = place_ref[0], place_ref[1]
    fetches = [pltpu.make_async_copy(r_hbm, r_ref, sems.at[3])]
    fetches += [pltpu.make_async_copy(g_hbm.at[:, :, a], g_ref.at[a], sems.at[4 + a]) for a in range(2)]
    for core, sources in enumerate(((mine_hbm, mine_hbm, other_hbm), (other_hbm, other_hbm, mine_hbm))):

        @pl.when(lax.rem(col, CORE) == core)
        def _():
            copies = [
                pltpu.make_async_copy(source.at[:, min(i, 1)], tiles_ref.at[i], sems.at[i])
                for i, source in enumerate(sources)
            ]
            for copy in copies:
                copy.start()
            for copy in copies:
                copy.wait()

    for fetch in fetches:
        fetch.start()
    for i, at in enumerate(((0, 0), (1, 0), (1, 1))):
        a_ref[at[0] * NB : (at[0] + 1) * NB, at[1] * NB : (at[1] + 1) * NB] = tiles_ref[i].reshape(NB, NB)

    def blk(i):
        return slice(i * LANE, (i + 1) * LANE)

    def panel(k, pair):
        if pair == 0:
            parts = [r_ref[:, k, a] for a in range(trd)]
        else:
            parts = [g_ref[pair - 1, 2 * h + k] for h in range(2)]
        return jnp.concatenate([part.reshape(NB, NB) for part in parts], 0)

    def rows_of(pair):
        return slice(pair * 2 * NB, (pair + 1) * 2 * NB)

    def keep(ref, rows, parts):
        for j, part in enumerate(parts):
            ref[j, rows] = part

    def parts_of(ref, rows):
        return [ref[j, rows] for j in range(3)]

    def tile_of(b):
        return slice((trd + b) * NB, (trd + b + 1) * NB)

    pairs = 1 + tcd // 2
    weights = {}

    def first_solve(pair):
        keep(s0_ref, rows_of(pair), split(dot6(split(panel(0, pair)), weights[0])))

    def second_panel(pair):
        keep(t_ref, rows_of(pair), split(panel(1, pair) - dot6(parts_of(s0_ref, rows_of(pair)), weights[1])))

    def first_update(b):
        u = dot6(parts_of(s0_ref, rows_of(0)), parts_of(s0_ref, tile_of(b)))
        for a in range(trd):
            out_ref[a, :, b, :] = cov_ref[a, :, b, :] - u[a * nb : (a + 1) * nb]

    work = []
    for pair in range(pairs):
        work.append((first_solve, pair))
    for pair in range(pairs):
        work.append((second_panel, pair))
    for b in range(tcd):
        work.append((first_update, b))
    ticks = [0]

    def nothing():
        pass

    def some_work():
        ticks[0] += 1
        if ticks[0] % 3 == 0 and work:
            step, index = work.pop(0)
            step(index)

    count = a_ref.shape[0] // LANE
    inverses = []
    for b in range(count):
        rows = [a_ref[b * LANE + SUB * g : b * LANE + SUB * (g + 1), blk(b)] for g in range(LANE // SUB)]
        upper, inverse = factor_block(rows, spread_ref, some_work if b > 1 else nothing)
        inverses.append(inverse)
        l_ref[blk(b), blk(b)] = upper
        for i in range(b + 1, count):
            below = dot_nt(a_ref[blk(i), blk(b)], inverse)
            l_ref[blk(i), blk(b)] = below
            for j in range(b + 1, i + 1):
                a_ref[blk(i), blk(j)] = a_ref[blk(i), blk(j)] - dot_nt(below, l_ref[blk(j), blk(b)])
        half, odd = divmod(b, 2)
        w_ref[half, blk(odd), blk(odd)] = inverse
        if odd:
            w_ref[half, blk(0), blk(1)] = jnp.zeros((LANE, LANE), jnp.float32)
            w_ref[half, blk(1), blk(0)] = -dot_nn(inverse, dot_nn(l_ref[blk(b), blk(b - 1)], inverses[b - 1]))
        if b == 1:
            weights[0], weights[1] = split(w_ref[0]), split(l_ref[NB:, :NB])
            for fetch in fetches:
                fetch.wait()
    while work:
        step, index = work.pop(0)
        step(index)
    last = split(w_ref[1])
    for pair in range(pairs):
        keep(s1_ref, rows_of(pair), split(dot6(parts_of(t_ref, rows_of(pair)), last)))
    for b in range(tcd):
        u = dot6(parts_of(s1_ref, rows_of(0)), parts_of(s1_ref, tile_of(b)))
        for a in range(trd):
            out_ref[a, :, b, :] = out_ref[a, :, b, :] - u[a * nb : (a + 1) * nb]

    for k, ref in enumerate((s0_ref, s1_ref)):

        @pl.when(col == k)
        def _():
            s = sum(ref[j, rows_of(0)].astype(jnp.float32) for j in (2, 1, 0))
            for a in range(trd):
                out_ref[a, :, 0, :] = s[a * nb : (a + 1) * nb]

    @pl.when(row < 2)
    def _():
        out_ref[0] = jnp.zeros_like(out_ref[0])

    for i in range(2):
        for j in range(i + 1):

            @pl.when(jnp.logical_and(row == i, col == j))
            def _():
                for u in range(2):
                    for v in range(2):
                        if i == j and u < v:
                            continue
                        block = l_ref[blk(2 * i + u), blk(2 * j + v)]
                        out_ref[0, blk(u), 0, blk(v)] = block.T if i == j and u == v else block


def head_and_update(place, cov, mine, other, r, g):
    trd, nb, tcd, _ = cov.shape
    n = 2 * NB
    vmem, hbm = (pl.BlockSpec(memory_space=space) for space in (pltpu.VMEM, pltpu.HBM))
    moved = [mine, other, r.reshape(Z, CORE, trd, PART, nb), g]
    moved = [pltpu.with_memory_space_constraint(array, pltpu.HBM) for array in moved]
    solved = pltpu.VMEM((3, (trd + tcd) * nb, nb), jnp.bfloat16)
    return pl.pallas_call(
        head_and_update_kernel,
        out_shape=jax.ShapeDtypeStruct(cov.shape, jnp.float32),
        in_specs=[pl.BlockSpec(memory_space=pltpu.SMEM), vmem] + [hbm] * len(moved),
        out_specs=vmem,
        scratch_shapes=[
            pltpu.VMEM((3, Z, PART, nb), jnp.float32),
            pltpu.VMEM((Z, CORE, trd, PART, nb), jnp.float32),
            pltpu.VMEM((2, X, Y, PART, nb), jnp.float32),
            pltpu.VMEM((n, n), jnp.float32),
            pltpu.VMEM((n, n), jnp.float32),
            pltpu.VMEM((2, nb, nb), jnp.float32),
            solved,
            solved,
            solved,
            pltpu.VMEM((2 * SUB * (SUB + 2), LANE), jnp.float32),
            pltpu.SemaphoreType.DMA((6,)),
        ],
        compiler_params=pltpu.CompilerParams(vmem_limit_bytes=32 * 2**20),
        name="update",
    )(place, cov, *moved)


def shared(block, groups):
    many = jnp.broadcast_to(block[None], (len(groups[0]),) + block.shape)
    return lax.all_to_all(many, "row", 0, 0, axis_index_groups=groups)


def on_device(cov):
    row, col = lax.axis_index("row"), lax.axis_index("col")
    x, z = row // Y, col // CORE
    panel = cov[:, :, 0, :].reshape(2, Z, PART, NB)

    mine = jnp.where(z == 0, panel[:, 0], 0.0)
    for s in range(1, Z):
        pairs = [(p * N_COL + k, p * N_COL + s * CORE + k) for p in range(N_ROW) for k in range(CORE)]
        mine = mine + lax.ppermute(panel[:, s], BOTH, pairs)
    r = lax.all_gather(mine, "col")

    head = jnp.where(x == 0, mine[0], 0.0)
    for s in range(1, X):
        pairs = [(device(0, y, c, k), device(s, y, c, k)) for c in range(Z) for y, k in ROOTS]
        head = head + lax.ppermute(mine[0], BOTH, pairs)

    pairs = [
        (p * N_COL + c * CORE + k, device(2 * (p // N_COL) + k, c, (p % N_COL) // CORE, p % CORE))
        for p in range(N_ROW)
        for c in range(Z)
        for k in range(CORE)
    ]
    mine = lax.ppermute(mine, BOTH, pairs)
    got = shared(jnp.concatenate([mine, head[None]]), [[i * Y + j for j in range(Y)] for i in range(X)])
    g = lax.all_gather(got[:, :2], "row", axis_index_groups=[[i * Y + j for i in range(X)] for j in range(Y)])

    many = jnp.broadcast_to(got[None, :2, 2], (Z, 2, PART, NB))
    tiles = lax.all_to_all(many, "col", 0, 0, axis_index_groups=[[c * CORE + k for c in range(Z)] for k in range(CORE)])
    other = lax.ppermute(tiles, "col", [(i, i ^ 1) for i in range(N_COL)])
    return head_and_update(jnp.stack([row, col]).astype(jnp.int32), cov, tiles, other, r, g)


def solution(mesh):
    placed = (P(None, "row", None, "col"),)
    return jax.shard_map(
        on_device,
        mesh=mesh,
        in_specs=placed,
        out_specs=P(None, "row", None, "col"),
        check_vma=False,
    )
```

```python
import jax
import jax.numpy as jnp
from jax import lax
from jax.experimental import pallas as pl
from jax.experimental.pallas import tpu as pltpu
from jax.sharding import PartitionSpec as P

LANE = 128
SUB = 8
X, Y, Z, CORE = 4, 8, 8, 2
N_ROW, N_COL = X * Y, Z * CORE
NB = 256
PART = NB // Z
BOTH = ("row", "col")


def device(x, y, z, core):
    return (x * Y + y) * N_COL + z * CORE + core


def dot_nt(a, b):
    return lax.dot_general(
        a, b, (((1,), (1,)), ((), ())), precision=lax.Precision.HIGHEST, preferred_element_type=jnp.float32
    )


def dot_nn(a, b):
    return lax.dot_general(
        a, b, (((1,), (0,)), ((), ())), precision=lax.Precision.HIGHEST, preferred_element_type=jnp.float32
    )


def column(rows, k):
    return jnp.broadcast_to(rows[:, k : k + 1], (SUB, LANE))


def total(terms):
    terms = list(terms)
    while len(terms) > 1:
        terms = [sum(terms[i : i + 2]) for i in range(0, len(terms), 2)]
    return terms[0]


def factor_block(rows, s_ref, between):
    count = len(rows)
    rows = list(rows)
    sub = lax.broadcasted_iota(jnp.int32, (SUB, LANE), 0)
    lane = lax.broadcasted_iota(jnp.int32, (SUB, LANE), 1)
    aug = [jnp.where(lane == sub + SUB * g, 1.0, 0.0).astype(jnp.float32) for g in range(count)]
    span = SUB * (SUB + 2)
    for p in range(count):
        base = (p % 2) * span
        for k in range(SUB):
            s_ref[base + SUB * k : base + SUB * (k + 1), :] = column(rows[p], SUB * p + k)
        s_ref[base + SUB * SUB : base + SUB * (SUB + 1), :] = rows[p]
        s_ref[base + SUB * (SUB + 1) : base + span, :] = aug[p]

        def spread(i, base=base):
            return jnp.broadcast_to(s_ref[base + i : base + i + 1, :], (SUB, LANE))

        a = {(m, k): spread(SUB * k + m) for k in range(SUB) for m in range(k, SUB)}
        low, scale = {}, []
        for k in range(0, SUB, 2):
            first, cross, second = a[k, k], a[k + 1, k], a[k + 1, k + 1]
            r1 = lax.rsqrt(first)
            r2 = lax.rsqrt(first * second - cross * cross) * (first * r1)
            scale += [r1, r2]
            low[k + 1, k] = cross * r1
            for m in range(k + 2, SUB):
                low[m, k] = a[m, k] * r1
                low[m, k + 1] = (a[m, k + 1] - low[m, k] * low[k + 1, k]) * r2
            for m in range(k + 2, SUB):
                for n in range(k + 2, m + 1):
                    a[m, n] = a[m, n] - (low[m, k] * low[n, k] + low[m, k + 1] * low[n, k + 1])
        xs, ys = [], []
        for k in range(SUB):
            x, y = spread(SUB * SUB + k), spread(SUB * (SUB + 1) + k)
            for j in range(k):
                x = x - low[k, j] * xs[j]
                y = y - low[k, j] * ys[j]
            xs.append(x * scale[k])
            ys.append(y * scale[k])
        for g in range(p + 1, count):
            left = []
            for k in range(SUB):
                t = column(rows[g], SUB * p + k)
                for j in range(k):
                    t = t - left[j] * low[k, j]
                left.append(t * scale[k])
            rows[g] = rows[g] - total(c * x for c, x in zip(left, xs))
            aug[g] = aug[g] - total(c * y for c, y in zip(left, ys))
        x, y = xs[0], ys[0]
        for k in range(1, SUB):
            x = jnp.where(sub == k, xs[k], x)
            y = jnp.where(sub == k, ys[k], y)
        rows[p] = jnp.where(lane >= sub + SUB * p, x, 0.0)
        aug[p] = y
        between()
    return jnp.concatenate(rows, 0), jnp.concatenate(aug, 0)


def split(x):
    hi = x.astype(jnp.bfloat16)
    rest = x - hi.astype(jnp.float32)
    mid = rest.astype(jnp.bfloat16)
    return hi, mid, (rest - mid.astype(jnp.float32)).astype(jnp.bfloat16)


def dot6(a, b):
    out = None
    for i in range(3):
        for j in range(3 - i):
            t = lax.dot_general(a[i], b[j], (((1,), (1,)), ((), ())), preferred_element_type=jnp.float32)
            out = t if out is None else out + t
    return out


def head_and_update_kernel(
    place_ref, cov_ref, mine_hbm, other_hbm, r_hbm, g_hbm, out_ref,
    tiles_ref, r_ref, g_ref, a_ref, l_ref, w_ref, s0_ref, t_ref, s1_ref, spread_ref, sems,
):
    trd, nb, tcd, _ = cov_ref.shape
    row, col = place_ref[0], place_ref[1]
    fetches = [pltpu.make_async_copy(r_hbm, r_ref, sems.at[3])]
    fetches += [pltpu.make_async_copy(g_hbm.at[:, :, a], g_ref.at[a], sems.at[4 + a]) for a in range(2)]
    for core, sources in enumerate(((mine_hbm, mine_hbm, other_hbm), (other_hbm, other_hbm, mine_hbm))):

        @pl.when(lax.rem(col, CORE) == core)
        def _():
            copies = [
                pltpu.make_async_copy(source.at[:, min(i, 1)], tiles_ref.at[i], sems.at[i])
                for i, source in enumerate(sources)
            ]
            for copy in copies:
                copy.start()
            for copy in copies:
                copy.wait()

    for fetch in fetches:
        fetch.start()
    for i, at in enumerate(((0, 0), (1, 0), (1, 1))):
        a_ref[at[0] * NB : (at[0] + 1) * NB, at[1] * NB : (at[1] + 1) * NB] = tiles_ref[i].reshape(NB, NB)

    def blk(i):
        return slice(i * LANE, (i + 1) * LANE)

    def panel(k, pair):
        if pair == 0:
            parts = [r_ref[:, k, a] for a in range(trd)]
        else:
            parts = [g_ref[pair - 1, 2 * h + k] for h in range(2)]
        return jnp.concatenate([part.reshape(NB, NB) for part in parts], 0)

    def rows_of(pair):
        return slice(pair * 2 * NB, (pair + 1) * 2 * NB)

    def keep(ref, rows, parts):
        for j, part in enumerate(parts):
            ref[j, rows] = part

    def parts_of(ref, rows):
        return [ref[j, rows] for j in range(3)]

    def tile_of(b):
        return slice((trd + b) * NB, (trd + b + 1) * NB)

    pairs = 1 + tcd // 2
    weights = {}

    def first_solve(pair):
        keep(s0_ref, rows_of(pair), split(dot6(split(panel(0, pair)), weights[0])))

    def second_panel(pair):
        keep(t_ref, rows_of(pair), split(panel(1, pair) - dot6(parts_of(s0_ref, rows_of(pair)), weights[1])))

    def first_update(b):
        u = dot6(parts_of(s0_ref, rows_of(0)), parts_of(s0_ref, tile_of(b)))
        for a in range(trd):
            out_ref[a, :, b, :] = cov_ref[a, :, b, :] - u[a * nb : (a + 1) * nb]

    work = []
    for pair in range(pairs):
        work.append((first_solve, pair))
    for pair in range(pairs):
        work.append((second_panel, pair))
    for b in range(tcd):
        work.append((first_update, b))
    ticks = [0]

    def nothing():
        pass

    def some_work():
        ticks[0] += 1
        if ticks[0] % 3 == 0 and work:
            step, index = work.pop(0)
            step(index)

    count = a_ref.shape[0] // LANE
    inverses = []
    for b in range(count):
        rows = [a_ref[b * LANE + SUB * g : b * LANE + SUB * (g + 1), blk(b)] for g in range(LANE // SUB)]
        upper, inverse = factor_block(rows, spread_ref, some_work if b > 1 else nothing)
        inverses.append(inverse)
        l_ref[blk(b), blk(b)] = upper
        for i in range(b + 1, count):
            below = dot_nt(a_ref[blk(i), blk(b)], inverse)
            l_ref[blk(i), blk(b)] = below
            for j in range(b + 1, i + 1):
                a_ref[blk(i), blk(j)] = a_ref[blk(i), blk(j)] - dot_nt(below, l_ref[blk(j), blk(b)])
        half, odd = divmod(b, 2)
        w_ref[half, blk(odd), blk(odd)] = inverse
        if odd:
            w_ref[half, blk(0), blk(1)] = jnp.zeros((LANE, LANE), jnp.float32)
            w_ref[half, blk(1), blk(0)] = -dot_nn(inverse, dot_nn(l_ref[blk(b), blk(b - 1)], inverses[b - 1]))
        if b == 1:
            weights[0], weights[1] = split(w_ref[0]), split(l_ref[NB:, :NB])
            for fetch in fetches:
                fetch.wait()
    while work:
        step, index = work.pop(0)
        step(index)
    last = split(w_ref[1])
    for pair in range(pairs):
        keep(s1_ref, rows_of(pair), split(dot6(parts_of(t_ref, rows_of(pair)), last)))
    for b in range(tcd):
        u = dot6(parts_of(s1_ref, rows_of(0)), parts_of(s1_ref, tile_of(b)))
        for a in range(trd):
            out_ref[a, :, b, :] = out_ref[a, :, b, :] - u[a * nb : (a + 1) * nb]

    for k, ref in enumerate((s0_ref, s1_ref)):

        @pl.when(col == k)
        def _():
            s = sum(ref[j, rows_of(0)].astype(jnp.float32) for j in (2, 1, 0))
            for a in range(trd):
                out_ref[a, :, 0, :] = s[a * nb : (a + 1) * nb]

    @pl.when(row < 2)
    def _():
        out_ref[0] = jnp.zeros_like(out_ref[0])

    for i in range(2):
        for j in range(i + 1):

            @pl.when(jnp.logical_and(row == i, col == j))
            def _():
                for u in range(2):
                    for v in range(2):
                        if i == j and u < v:
                            continue
                        block = l_ref[blk(2 * i + u), blk(2 * j + v)]
                        out_ref[0, blk(u), 0, blk(v)] = block.T if i == j and u == v else block


def head_and_update(place, cov, mine, other, r, g):
    trd, nb, tcd, _ = cov.shape
    n = 2 * NB
    vmem, hbm = (pl.BlockSpec(memory_space=space) for space in (pltpu.VMEM, pltpu.HBM))
    moved = [mine, other, r.reshape(Z, CORE, trd, PART, nb), g]
    moved = [pltpu.with_memory_space_constraint(array, pltpu.HBM) for array in moved]
    solved = pltpu.VMEM((3, (trd + tcd) * nb, nb), jnp.bfloat16)
    return pl.pallas_call(
        head_and_update_kernel,
        out_shape=jax.ShapeDtypeStruct(cov.shape, jnp.float32),
        in_specs=[pl.BlockSpec(memory_space=pltpu.SMEM), vmem] + [hbm] * len(moved),
        out_specs=vmem,
        scratch_shapes=[
            pltpu.VMEM((3, Z, PART, nb), jnp.float32),
            pltpu.VMEM((Z, CORE, trd, PART, nb), jnp.float32),
            pltpu.VMEM((2, X, Y, PART, nb), jnp.float32),
            pltpu.VMEM((n, n), jnp.float32),
            pltpu.VMEM((n, n), jnp.float32),
            pltpu.VMEM((2, nb, nb), jnp.float32),
            solved,
            solved,
            solved,
            pltpu.VMEM((2 * SUB * (SUB + 2), LANE), jnp.float32),
            pltpu.SemaphoreType.DMA((6,)),
        ],
        compiler_params=pltpu.CompilerParams(vmem_limit_bytes=32 * 2**20),
        name="update",
    )(place, cov, *moved)


def shared(block, groups):
    many = jnp.broadcast_to(block[None], (len(groups[0]),) + block.shape)
    return lax.all_to_all(many, "row", 0, 0, axis_index_groups=groups)


def on_device(cov):
    row, col = lax.axis_index("row"), lax.axis_index("col")
    x, z = row // Y, col // CORE
    panel = cov[:, :, 0, :].reshape(2, Z, PART, NB)

    mine = jnp.where(z == 0, panel[:, 0], 0.0)
    for s in range(1, Z):
        pairs = [(p * N_COL + k, p * N_COL + s * CORE + k) for p in range(N_ROW) for k in range(CORE)]
        mine = mine + lax.ppermute(panel[:, s], BOTH, pairs)
    r = lax.all_gather(mine, "col")

    pairs = [
        (p * N_COL + c * CORE + k, device(2 * (p // N_COL) + k, c, (p % N_COL) // CORE, p % CORE))
        for p in range(N_ROW)
        for c in range(Z)
        for k in range(CORE)
    ]
    moved = lax.ppermute(mine, BOTH, pairs)
    got = shared(jnp.concatenate([moved, mine[:1]]), [[i * Y + j for j in range(Y)] for i in range(X)])
    g = lax.all_gather(got[:, :2], "row", axis_index_groups=[[i * Y + j for i in range(X)] for j in range(Y)])

    head = jnp.where(x == 0, got[:2, 2], 0.0)
    for s in range(1, X):
        pairs = [(device(0, y, c, k), device(s, y, c, k)) for y in range(Y) for c in range(Z) for k in range(CORE)]
        head = head + lax.ppermute(got[:2, 2], BOTH, pairs)
    many = jnp.broadcast_to(head[None], (Z, 2, PART, NB))
    tiles = lax.all_to_all(many, "col", 0, 0, axis_index_groups=[[c * CORE + k for c in range(Z)] for k in range(CORE)])
    other = lax.ppermute(tiles, "col", [(i, i ^ 1) for i in range(N_COL)])
    return head_and_update(jnp.stack([row, col]).astype(jnp.int32), cov, tiles, other, r, g)


def solution(mesh):
    placed = (P(None, "row", None, "col"),)
    return jax.shard_map(
        on_device,
        mesh=mesh,
        in_specs=placed,
        out_specs=P(None, "row", None, "col"),
        check_vma=False,
    )
```

```python
import jax
import jax.numpy as jnp
from jax import lax
from jax.experimental import pallas as pl
from jax.experimental.pallas import tpu as pltpu
from jax.sharding import PartitionSpec as P

LANE = 128
SUB = 8
X, Y, Z, CORE = 4, 8, 8, 2
N_ROW, N_COL = X * Y, Z * CORE
NB = 256
PART = NB // Z
BOTH = ("row", "col")
ROOTS = ((0, 0), (1, 0), (1, 1))


def device(x, y, z, core):
    return (x * Y + y) * N_COL + z * CORE + core


def dot_nt(a, b):
    return lax.dot_general(
        a, b, (((1,), (1,)), ((), ())), precision=lax.Precision.HIGHEST, preferred_element_type=jnp.float32
    )


def dot_nn(a, b):
    return lax.dot_general(
        a, b, (((1,), (0,)), ((), ())), precision=lax.Precision.HIGHEST, preferred_element_type=jnp.float32
    )


def column(rows, k):
    return jnp.broadcast_to(rows[:, k : k + 1], (SUB, LANE))


def total(terms):
    terms = list(terms)
    while len(terms) > 1:
        terms = [sum(terms[i : i + 2]) for i in range(0, len(terms), 2)]
    return terms[0]


def factor_block(rows, s_ref, between):
    count = len(rows)
    rows = list(rows)
    sub = lax.broadcasted_iota(jnp.int32, (SUB, LANE), 0)
    lane = lax.broadcasted_iota(jnp.int32, (SUB, LANE), 1)
    aug = [jnp.where(lane == sub + SUB * g, 1.0, 0.0).astype(jnp.float32) for g in range(count)]
    span = SUB * (SUB + 2)
    for p in range(count):
        base = (p % 2) * span
        for k in range(SUB):
            s_ref[base + SUB * k : base + SUB * (k + 1), :] = column(rows[p], SUB * p + k)
        s_ref[base + SUB * SUB : base + SUB * (SUB + 1), :] = rows[p]
        s_ref[base + SUB * (SUB + 1) : base + span, :] = aug[p]

        def spread(i, base=base):
            return jnp.broadcast_to(s_ref[base + i : base + i + 1, :], (SUB, LANE))

        a = {(m, k): spread(SUB * k + m) for k in range(SUB) for m in range(k, SUB)}
        low, scale = {}, []
        for k in range(0, SUB, 2):
            first, cross, second = a[k, k], a[k + 1, k], a[k + 1, k + 1]
            r1 = lax.rsqrt(first)
            r2 = lax.rsqrt(first * second - cross * cross) * (first * r1)
            scale += [r1, r2]
            low[k + 1, k] = cross * r1
            for m in range(k + 2, SUB):
                low[m, k] = a[m, k] * r1
                low[m, k + 1] = (a[m, k + 1] - low[m, k] * low[k + 1, k]) * r2
            for m in range(k + 2, SUB):
                for n in range(k + 2, m + 1):
                    a[m, n] = a[m, n] - (low[m, k] * low[n, k] + low[m, k + 1] * low[n, k + 1])
        xs, ys = [], []
        for k in range(SUB):
            x, y = spread(SUB * SUB + k), spread(SUB * (SUB + 1) + k)
            for j in range(k):
                x = x - low[k, j] * xs[j]
                y = y - low[k, j] * ys[j]
            xs.append(x * scale[k])
            ys.append(y * scale[k])
        for g in range(p + 1, count):
            left = []
            for k in range(SUB):
                t = column(rows[g], SUB * p + k)
                for j in range(k):
                    t = t - left[j] * low[k, j]
                left.append(t * scale[k])
            rows[g] = rows[g] - total(c * x for c, x in zip(left, xs))
            aug[g] = aug[g] - total(c * y for c, y in zip(left, ys))
        x, y = xs[0], ys[0]
        for k in range(1, SUB):
            x = jnp.where(sub == k, xs[k], x)
            y = jnp.where(sub == k, ys[k], y)
        rows[p] = jnp.where(lane >= sub + SUB * p, x, 0.0)
        aug[p] = y
        between()
    return jnp.concatenate(rows, 0), jnp.concatenate(aug, 0)


def split(x):
    hi = x.astype(jnp.bfloat16)
    rest = x - hi.astype(jnp.float32)
    mid = rest.astype(jnp.bfloat16)
    return hi, mid, (rest - mid.astype(jnp.float32)).astype(jnp.bfloat16)


def dot6(a, b):
    out = None
    for i in range(3):
        for j in range(3 - i):
            t = lax.dot_general(a[i], b[j], (((1,), (1,)), ((), ())), preferred_element_type=jnp.float32)
            out = t if out is None else out + t
    return out


def head_and_update_kernel(
    place_ref, cov_ref, mine_hbm, other_hbm, r_hbm, g_hbm, out_ref,
    tiles_ref, r_ref, g_ref, a_ref, l_ref, w_ref, s0_ref, t_ref, s1_ref, spread_ref, sems,
):
    trd, nb, tcd, _ = cov_ref.shape
    row, col = place_ref[0], place_ref[1]
    fetches = [pltpu.make_async_copy(r_hbm, r_ref, sems.at[3])]
    fetches += [pltpu.make_async_copy(g_hbm.at[:, :, a], g_ref.at[a], sems.at[4 + a]) for a in range(2)]
    for core, sources in enumerate(((mine_hbm, mine_hbm, other_hbm), (other_hbm, other_hbm, mine_hbm))):

        @pl.when(lax.rem(col, CORE) == core)
        def _():
            copies = [
                pltpu.make_async_copy(source.at[:, min(i, 1)], tiles_ref.at[i], sems.at[i])
                for i, source in enumerate(sources)
            ]
            for copy in copies:
                copy.start()
            for copy in copies:
                copy.wait()

    for fetch in fetches:
        fetch.start()
    for i, at in enumerate(((0, 0), (1, 0), (1, 1))):
        a_ref[at[0] * NB : (at[0] + 1) * NB, at[1] * NB : (at[1] + 1) * NB] = tiles_ref[i].reshape(NB, NB)

    def blk(i):
        return slice(i * LANE, (i + 1) * LANE)

    def panel(k, pair):
        if pair == 0:
            parts = [r_ref[:, k, a] for a in range(trd)]
        else:
            parts = [g_ref[pair - 1, 2 * h + k] for h in range(2)]
        return jnp.concatenate([part.reshape(NB, NB) for part in parts], 0)

    def rows_of(pair):
        return slice(pair * 2 * NB, (pair + 1) * 2 * NB)

    def keep(ref, rows, parts):
        for j, part in enumerate(parts):
            ref[j, rows] = part

    def parts_of(ref, rows):
        return [ref[j, rows] for j in range(3)]

    def tile_of(b):
        return slice((trd + b) * NB, (trd + b + 1) * NB)

    pairs = 1 + tcd // 2
    weights = {}

    def first_solve(pair):
        keep(s0_ref, rows_of(pair), split(dot6(split(panel(0, pair)), weights[0])))

    def second_panel(pair):
        keep(t_ref, rows_of(pair), split(panel(1, pair) - dot6(parts_of(s0_ref, rows_of(pair)), weights[1])))

    def first_update(b):
        u = dot6(parts_of(s0_ref, rows_of(0)), parts_of(s0_ref, tile_of(b)))
        for a in range(trd):
            out_ref[a, :, b, :] = cov_ref[a, :, b, :] - u[a * nb : (a + 1) * nb]

    work = []
    for pair in range(pairs):
        work.append((first_solve, pair))
    for pair in range(pairs):
        work.append((second_panel, pair))
    for b in range(tcd):
        work.append((first_update, b))
    ticks = [0]

    def nothing():
        pass

    def some_work():
        ticks[0] += 1
        if ticks[0] % 3 == 0 and work:
            step, index = work.pop(0)
            step(index)

    count = a_ref.shape[0] // LANE
    inverses = []
    for b in range(count):
        rows = [a_ref[b * LANE + SUB * g : b * LANE + SUB * (g + 1), blk(b)] for g in range(LANE // SUB)]
        upper, inverse = factor_block(rows, spread_ref, some_work if b > 1 else nothing)
        inverses.append(inverse)
        l_ref[blk(b), blk(b)] = upper
        for i in range(b + 1, count):
            below = dot_nt(a_ref[blk(i), blk(b)], inverse)
            l_ref[blk(i), blk(b)] = below
            for j in range(b + 1, i + 1):
                a_ref[blk(i), blk(j)] = a_ref[blk(i), blk(j)] - dot_nt(below, l_ref[blk(j), blk(b)])
        half, odd = divmod(b, 2)
        w_ref[half, blk(odd), blk(odd)] = inverse
        if odd:
            w_ref[half, blk(0), blk(1)] = jnp.zeros((LANE, LANE), jnp.float32)
            w_ref[half, blk(1), blk(0)] = -dot_nn(inverse, dot_nn(l_ref[blk(b), blk(b - 1)], inverses[b - 1]))
        if b == 1:
            weights[0], weights[1] = split(w_ref[0]), split(l_ref[NB:, :NB])
            for fetch in fetches:
                fetch.wait()
    while work:
        step, index = work.pop(0)
        step(index)
    last = split(w_ref[1])
    for pair in range(pairs):
        keep(s1_ref, rows_of(pair), split(dot6(parts_of(t_ref, rows_of(pair)), last)))
    for b in range(tcd):
        u = dot6(parts_of(s1_ref, rows_of(0)), parts_of(s1_ref, tile_of(b)))
        for a in range(trd):
            out_ref[a, :, b, :] = out_ref[a, :, b, :] - u[a * nb : (a + 1) * nb]

    for k, ref in enumerate((s0_ref, s1_ref)):

        @pl.when(col == k)
        def _():
            s = sum(ref[j, rows_of(0)].astype(jnp.float32) for j in (2, 1, 0))
            for a in range(trd):
                out_ref[a, :, 0, :] = s[a * nb : (a + 1) * nb]

    @pl.when(row < 2)
    def _():
        out_ref[0] = jnp.zeros_like(out_ref[0])

    for i in range(2):
        for j in range(i + 1):

            @pl.when(jnp.logical_and(row == i, col == j))
            def _():
                for u in range(2):
                    for v in range(2):
                        if i == j and u < v:
                            continue
                        block = l_ref[blk(2 * i + u), blk(2 * j + v)]
                        out_ref[0, blk(u), 0, blk(v)] = block.T if i == j and u == v else block


def head_and_update(place, cov, mine, other, r, g):
    trd, nb, tcd, _ = cov.shape
    n = 2 * NB
    vmem, hbm = (pl.BlockSpec(memory_space=space) for space in (pltpu.VMEM, pltpu.HBM))
    moved = [mine, other, r.reshape(Z, CORE, trd, PART, nb), g]
    moved = [pltpu.with_memory_space_constraint(array, pltpu.HBM) for array in moved]
    solved = pltpu.VMEM((3, (trd + tcd) * nb, nb), jnp.bfloat16)
    return pl.pallas_call(
        head_and_update_kernel,
        out_shape=jax.ShapeDtypeStruct(cov.shape, jnp.float32),
        in_specs=[pl.BlockSpec(memory_space=pltpu.SMEM), vmem] + [hbm] * len(moved),
        out_specs=vmem,
        scratch_shapes=[
            pltpu.VMEM((3, Z, PART, nb), jnp.float32),
            pltpu.VMEM((Z, CORE, trd, PART, nb), jnp.float32),
            pltpu.VMEM((2, X, Y, PART, nb), jnp.float32),
            pltpu.VMEM((n, n), jnp.float32),
            pltpu.VMEM((n, n), jnp.float32),
            pltpu.VMEM((2, nb, nb), jnp.float32),
            solved,
            solved,
            solved,
            pltpu.VMEM((2 * SUB * (SUB + 2), LANE), jnp.float32),
            pltpu.SemaphoreType.DMA((6,)),
        ],
        compiler_params=pltpu.CompilerParams(vmem_limit_bytes=32 * 2**20),
        name="update",
    )(place, cov, *moved)


def shared(block, groups):
    many = jnp.broadcast_to(block[None], (len(groups[0]),) + block.shape)
    return lax.all_to_all(many, "row", 0, 0, axis_index_groups=groups)


def on_device(cov):
    row, col = lax.axis_index("row"), lax.axis_index("col")
    x, z = row // Y, col // CORE
    panel = cov[:, :, 0, :].reshape(2, Z, PART, NB)

    mine = jnp.where(z == 0, panel[:, 0], 0.0)
    for s in range(1, Z):
        pairs = [(p * N_COL + k, p * N_COL + s * CORE + k) for p in range(N_ROW) for k in range(CORE)]
        mine = mine + lax.ppermute(panel[:, s], BOTH, pairs)
    r = lax.all_gather(mine, "col")

    head = jnp.where(x == 0, mine[0], 0.0)
    for s in (X // 2, 1):
        sources = range(0, X, 2 * s)
        pairs = [(device(i, y, c, k), device(i + s, y, c, k)) for i in sources for c in range(Z) for y, k in ROOTS]
        head = head + lax.ppermute(head, BOTH, pairs)

    pairs = [
        (p * N_COL + c * CORE + k, device(2 * (p // N_COL) + k, c, (p % N_COL) // CORE, p % CORE))
        for p in range(N_ROW)
        for c in range(Z)
        for k in range(CORE)
    ]
    mine = lax.ppermute(mine, BOTH, pairs)
    got = shared(jnp.concatenate([mine, head[None]]), [[i * Y + j for j in range(Y)] for i in range(X)])
    g = lax.all_gather(got[:, :2], "row", axis_index_groups=[[i * Y + j for i in range(X)] for j in range(Y)])

    many = jnp.broadcast_to(got[None, :2, 2], (Z, 2, PART, NB))
    tiles = lax.all_to_all(many, "col", 0, 0, axis_index_groups=[[c * CORE + k for c in range(Z)] for k in range(CORE)])
    other = lax.ppermute(tiles, "col", [(i, i ^ 1) for i in range(N_COL)])
    return head_and_update(jnp.stack([row, col]).astype(jnp.int32), cov, tiles, other, r, g)


def solution(mesh):
    placed = (P(None, "row", None, "col"),)
    return jax.shard_map(
        on_device,
        mesh=mesh,
        in_specs=placed,
        out_specs=P(None, "row", None, "col"),
        check_vma=False,
    )
```
